32 devices in a mesh: seq: 16 (over z, y, core), batch: 2 (over x).
Axes of the slice: x: 2, y: 2, z: 4, core: 2. Of those that a mesh axis runs over, the one named last changes fastest.
Arguments:
- coarse: bfloat16 [2, 4096, 1536], P('batch', 'seq'), may hold values from -6 to 6
- skip: bfloat16 [2, 8192, 1536], P('batch', 'seq'), may hold values from -6 to 6
- depth_kernel: float32 [3, 1536], replicated, may hold values from -3.5 to 3.5
- sep_weight: bfloat16 [1536, 1536], P('seq'), may hold values from -0.15625 to 0.15625
- sep_bias: float32 [1536], replicated, may hold values from -3 to 3
- head_weight: bfloat16 [1536, 3840], P(None, 'seq'), may hold values from -0.15625 to 0.15625
- head_bias: float32 [3840], replicated, may hold values from -4 to 4
- strand_pair: int32 [3840], replicated, may hold values from 0 to 3839, as said below
Outputs:
- preds: bfloat16 [2, 8192, 3840], P('batch', 'seq')
The draws below stay inside these ranges and needn't reach their ends.
Inputs may be any that keep to these rules, and one draw needn't show every extreme that they name: strand_pair is a permutation with strand_pair[strand_pair[t]] == t; about half of the tracks are paired with another one.
All inputs are finite; a program needn't handle non-finite values.
Results may differ from the reference program's by a relative error of at most 0.0053.
Values may be sent and summed in bfloat16 or wider, within the bound.
No kernel may reach another device: no remote copies, remote signals or barrier semaphores. Data moves between devices by JAX's collectives and lax.ppermute only.
A program may use at most 64 MiB of HBM per device.

```python
import jax
import jax.numpy as jnp
from jax import lax

D = 1536
TRACKS = 3840
NB = 8192
NC = 4096
SEQS = 1
ROWS = 2


def draw_strand_pair(key, part):
    order = jax.random.permutation(key, TRACKS).astype(jnp.int32)
    paired = TRACKS // 4
    first_half = order[:paired]
    second_half = order[paired:2 * paired]
    table = jnp.arange(TRACKS, dtype=jnp.int32)
    table = table.at[first_half].set(second_half).at[second_half].set(first_half)
    return table.astype(jnp.int32)


def steps_of(key, shape, cuts, least, high):
    def one(dim, parts):
        draws = jax.random.uniform(jax.random.fold_in(jax.random.fold_in(key, 6), dim), (parts,), jnp.float32, least / len(cuts), high / len(cuts))
        return jnp.repeat(jnp.exp(draws), shape[dim] // parts).reshape((-1,) + (1,) * (len(shape) - dim - 1))

    gain = one(*cuts[0])
    for cut in cuts[1:]:
        gain = gain * one(*cut)
    return gain


def gaussian(key, dims, spread, limit, split=(), kind=jnp.bfloat16):
    loudness = steps_of(key, dims, split, -0.22, 0.18) if split else 1.0
    result = jax.random.normal(key, dims, jnp.float32) * spread * loudness
    return jnp.minimum(jnp.maximum(result, -limit), limit).astype(kind)


def setup_inputs(seed: int = 0) -> dict:
    key_of = jax.random.split(jax.random.key(seed), 9)
    coarse = gaussian(key_of[0], (ROWS, NC, D), 1.0, 6.0, ((0, 2), (1, 16)))
    skip = gaussian(key_of[1], (ROWS, NB, D), 1.0, 6.0, ((0, 2), (1, 16)))
    depth_kernel = gaussian(key_of[2], (3, D), 3 ** -0.5, 3.5, (), jnp.float32)
    sep_weight = gaussian(key_of[3], (D, D), D ** -0.5, 0.15625, ((0, 16),))
    sep_bias = gaussian(key_of[4], (D,), 0.5, 3.0, (), jnp.float32)
    head_weight = gaussian(key_of[5], (D, TRACKS), D ** -0.5, 0.15625, ((1, 16),))
    head_bias = gaussian(key_of[6], (TRACKS,), 1.0, 4.0, (), jnp.float32)
    strand_pair = draw_strand_pair(jax.random.fold_in(key_of[8], 71), 0)
    return dict(coarse=coarse, skip=skip, depth_kernel=depth_kernel, sep_weight=sep_weight, sep_bias=sep_bias, head_weight=head_weight, head_bias=head_bias, strand_pair=strand_pair)


def strand_head(inputs, depth_kernel, sep_weight, sep_bias, head_weight, head_bias):
    coarse_row, skip_row = inputs
    upsampled = jnp.repeat(coarse_row.astype(jnp.float32), 2, axis=0)
    merged = (upsampled + skip_row.astype(jnp.float32)).astype(jnp.bfloat16)
    padded = jnp.pad(merged, ((1, 1), (0, 0)))
    depthwise = depth_kernel[0] * padded[:-2] + depth_kernel[1] * padded[1:-1] + depth_kernel[2] * padded[2:]
    depthwise = depthwise.astype(jnp.bfloat16)
    pointwise = jnp.dot(depthwise, sep_weight, preferred_element_type=jnp.float32) + sep_bias
    features = jax.nn.gelu(pointwise, approximate=True).astype(jnp.bfloat16)
    logits = jnp.dot(features, head_weight, preferred_element_type=jnp.float32) + head_bias
    return jax.nn.softplus(logits).astype(jnp.bfloat16)


def reference(coarse, skip, depth_kernel, sep_weight, sep_bias, head_weight, head_bias, strand_pair):
    strand_heads = lax.map(lambda inputs: strand_head(inputs, depth_kernel, sep_weight, sep_bias, head_weight, head_bias), (coarse, skip))
    partner = jnp.concatenate([strand_heads[SEQS:], strand_heads[:SEQS]], axis=0)
    partner = jnp.take(partner[:, ::-1], strand_pair, axis=2)
    averaged = 0.5 * (strand_heads.astype(jnp.float32) + partner.astype(jnp.float32))
    return averaged.astype(jnp.bfloat16)
```

```python
import functools

import jax
import jax.numpy as jnp
from jax import lax
from jax.experimental import pallas as pl
from jax.experimental.pallas import tpu as pltpu
from jax.sharding import PartitionSpec as P

BOTH = ("seq", "batch")
VMEM_LIMIT = 56 * 1024 * 1024


def params():
    return pltpu.CompilerParams(vmem_limit_bytes=VMEM_LIMIT)


def route(seq, batch, move):
    pairs = []
    for s in range(seq):
        for b in range(batch):
            target = move(s, b)
            if target is not None:
                pairs.append((s * batch + b, target[0] * batch + target[1]))
    return pairs


def send(array, move):
    seq, batch = lax.axis_size("seq"), lax.axis_size("batch")
    return lax.ppermute(array, BOTH, route(seq, batch, move))


def one_hot(shape, hit):
    rows = lax.broadcasted_iota(jnp.int32, shape, 0)
    columns = lax.broadcasted_iota(jnp.int32, shape, 1)
    return jnp.where(hit(rows, columns), 1.0, 0.0).astype(jnp.bfloat16)


def conv_kernel(coarse, skip, top, bottom, taps, own, flipped):
    bins = skip.shape[0]
    spread = one_hot((bins, coarse.shape[0]), lambda r, c: r // 2 == c)
    up = jnp.dot(spread, coarse[...], preferred_element_type=jnp.float32)
    merged = (up + skip[...].astype(jnp.float32)).astype(jnp.bfloat16).astype(jnp.float32)
    row = lax.broadcasted_iota(jnp.int32, merged.shape, 0)
    before = jnp.where(row == 0, top[...].astype(jnp.float32), pltpu.roll(merged, 1, 0))
    after = jnp.where(
        row == bins - 1, bottom[...].astype(jnp.float32), pltpu.roll(merged, bins - 1, 0)
    )
    result = taps[0:1, :] * before + taps[1:2, :] * merged + taps[2:3, :] * after
    result = result.astype(jnp.bfloat16)
    own[...] = result
    mirror = one_hot((bins, bins), lambda r, c: r + c == bins - 1)
    flipped[...] = jnp.dot(mirror, result, preferred_element_type=jnp.float32).astype(jnp.bfloat16)


def conv(coarse, skip, top, bottom, taps):
    bins, width = skip.shape
    step = 256
    column = lambda rows: pl.BlockSpec((rows, step), lambda j: (0, j))
    return pl.pallas_call(
        conv_kernel,
        grid=(width // step,),
        in_specs=[column(coarse.shape[0]), column(bins), column(1), column(1), column(3)],
        out_specs=[column(bins), column(bins)],
        out_shape=[jax.ShapeDtypeStruct((bins, width), jnp.bfloat16)] * 2,
        compiler_params=params(),
        name="conv",
    )(coarse, skip, top, bottom, taps)


def features_kernel(own, other, weight, bias, out):
    bins = own.shape[0]
    for place, part in enumerate((own, other)):
        product = jnp.dot(part[...], weight[...], preferred_element_type=jnp.float32)
        out[pl.ds(place * bins, bins), :] = jax.nn.gelu(
            product + bias[...], approximate=True
        ).astype(jnp.bfloat16)


def features(own, other, weight, bias):
    bins, width = own.shape
    step = 256
    whole = pl.BlockSpec((bins, width), lambda j: (0, 0))
    return pl.pallas_call(
        features_kernel,
        grid=(width // step,),
        in_specs=[
            whole,
            whole,
            pl.BlockSpec((width, step), lambda j: (0, j)),
            pl.BlockSpec((1, step), lambda j: (0, j)),
        ],
        out_specs=pl.BlockSpec((2 * bins, step), lambda j: (0, j)),
        out_shape=jax.ShapeDtypeStruct((2 * bins, width), jnp.bfloat16),
        compiler_params=params(),
        name="features",
    )(own, other, weight, bias)


def softplus(v):
    return jnp.maximum(v, 0.0) + jnp.log1p(jnp.exp(-jnp.abs(v)))


def heads_kernel(values, weight, bias, out):
    product = lax.dot_general(
        values[...], weight[...], (((1,), (1,)), ((), ())), preferred_element_type=jnp.float32
    )
    out[...] = softplus(product + bias[...]).astype(jnp.bfloat16)


def heads(values, weight, bias):
    rows, width = values.shape
    tracks = weight.shape[0]
    step = 256
    return pl.pallas_call(
        heads_kernel,
        grid=(tracks // step,),
        in_specs=[
            pl.BlockSpec((rows, width), lambda j: (0, 0)),
            pl.BlockSpec((step, width), lambda j: (j, 0)),
            pl.BlockSpec((1, step), lambda j: (0, j)),
        ],
        out_specs=pl.BlockSpec((rows, step), lambda j: (0, j)),
        out_shape=jax.ShapeDtypeStruct((rows, tracks), jnp.bfloat16),
        compiler_params=params(),
        name="heads",
    )(values, weight, bias)


def average_kernel(own, other, pair, out):
    tracks = other.shape[1]
    rows = lax.broadcasted_iota(jnp.int32, (tracks, pair.shape[1]), 0)
    chosen = jnp.where(rows == pair[...], 1.0, 0.0).astype(jnp.bfloat16)
    received = jnp.dot(other[...], chosen, preferred_element_type=jnp.float32)
    out[...] = (0.5 * (own[...].astype(jnp.float32) + received)).astype(jnp.bfloat16)


def average(both, pair):
    rows, tracks = both.shape
    bins = rows // 2
    step = 256
    return pl.pallas_call(
        average_kernel,
        grid=(tracks // step,),
        in_specs=[
            pl.BlockSpec((bins, step), lambda j: (0, j)),
            pl.BlockSpec((bins, tracks), lambda j: (1, 0)),
            pl.BlockSpec((1, step), lambda j: (0, j)),
        ],
        out_specs=pl.BlockSpec((bins, step), lambda j: (0, j)),
        out_shape=jax.ShapeDtypeStruct((bins, tracks), jnp.bfloat16),
        compiler_params=params(),
        name="average",
    )(both, both, pair)


def gather_rows(shard):
    batch = lax.axis_size("batch")
    part = shard.shape[0] // batch
    mine = lax.dynamic_slice_in_dim(shard, lax.axis_index("batch") * part, part, axis=0)
    return lax.all_gather(mine, BOTH, axis=0, tiled=True)


def edge(coarse_row, skip_row):
    total = coarse_row.astype(jnp.float32) + skip_row.astype(jnp.float32)
    return total.astype(jnp.bfloat16)


def per_device(
    coarse, skip, depth_kernel, sep_weight, sep_bias, head_weight, head_bias, strand_pair
):
    seq, batch = lax.axis_size("seq"), lax.axis_size("batch")
    coarse, skip = coarse[0], skip[0]
    first = edge(coarse[:1], skip[:1])
    last = edge(coarse[-1:], skip[-1:])
    top = send(last, lambda s, b: (s + 1, b) if s + 1 < seq else None)
    bottom = send(first, lambda s, b: (s - 1, b) if s > 0 else None)
    own, flipped = conv(coarse, skip, top, bottom, depth_kernel)
    other = send(flipped, lambda s, b: (seq - 1 - s, (b + batch // 2) % batch))
    values = features(own, other, gather_rows(sep_weight), sep_bias[None])
    both = heads(values, gather_rows(head_weight.T), head_bias[None])
    return average(both, strand_pair[None])[None]


def solution(mesh):
    in_specs = (
        P("batch", "seq", None),
        P("batch", "seq", None),
        P(),
        P("seq", None),
        P(),
        P(None, "seq"),
        P(),
        P(),
    )
    out_specs = P("batch", "seq", None)
    return jax.shard_map(
        per_device, mesh=mesh, in_specs=in_specs, out_specs=out_specs, check_vma=False
    )
```

```python
import functools

import jax
import jax.numpy as jnp
from jax import lax
from jax.experimental import pallas as pl
from jax.experimental.pallas import tpu as pltpu
from jax.sharding import PartitionSpec as P

BOTH = ("seq", "batch")
VMEM_LIMIT = 56 * 1024 * 1024


def params():
    return pltpu.CompilerParams(vmem_limit_bytes=VMEM_LIMIT)


def cost(flops, bytes_accessed):
    return pl.CostEstimate(flops=flops, bytes_accessed=bytes_accessed, transcendentals=0)


def route(seq, batch, move):
    pairs = []
    for s in range(seq):
        for b in range(batch):
            target = move(s, b)
            if target is not None:
                pairs.append((s * batch + b, target[0] * batch + target[1]))
    return pairs


def send(array, move):
    seq, batch = lax.axis_size("seq"), lax.axis_size("batch")
    return lax.ppermute(array, BOTH, route(seq, batch, move))


def one_hot(shape, hit):
    rows = lax.broadcasted_iota(jnp.int32, shape, 0)
    columns = lax.broadcasted_iota(jnp.int32, shape, 1)
    return jnp.where(hit(rows, columns), 1.0, 0.0).astype(jnp.bfloat16)


def conv_kernel(coarse, skip, top, bottom, taps, own, flipped):
    bins = skip.shape[0]
    spread = one_hot((bins, coarse.shape[0]), lambda r, c: r // 2 == c)
    up = jnp.dot(spread, coarse[...], preferred_element_type=jnp.float32)
    merged = (up + skip[...].astype(jnp.float32)).astype(jnp.bfloat16).astype(jnp.float32)
    row = lax.broadcasted_iota(jnp.int32, merged.shape, 0)
    before = jnp.where(row == 0, top[...].astype(jnp.float32), pltpu.roll(merged, 1, 0))
    after = jnp.where(
        row == bins - 1, bottom[...].astype(jnp.float32), pltpu.roll(merged, bins - 1, 0)
    )
    result = taps[0:1, :] * before + taps[1:2, :] * merged + taps[2:3, :] * after
    result = result.astype(jnp.bfloat16)
    own[...] = result
    mirror = one_hot((bins, bins), lambda r, c: r + c == bins - 1)
    flipped[...] = jnp.dot(mirror, result, preferred_element_type=jnp.float32).astype(jnp.bfloat16)


def conv(coarse, skip, top, bottom, taps):
    bins, width = skip.shape
    step = 256
    column = lambda rows: pl.BlockSpec((rows, step), lambda j: (0, j))
    return pl.pallas_call(
        conv_kernel,
        grid=(width // step,),
        in_specs=[column(coarse.shape[0]), column(bins), column(1), column(1), column(3)],
        out_specs=[column(bins), column(bins)],
        out_shape=[jax.ShapeDtypeStruct((bins, width), jnp.bfloat16)] * 2,
        compiler_params=params(),
        cost_estimate=cost(2 * bins * bins * width, 6 * bins * width),
        name="conv",
    )(coarse, skip, top, bottom, taps)


def softplus(v):
    e = jnp.exp(-jnp.abs(v))
    return jnp.maximum(v, 0.0) + jnp.where(e < 1e-4, e, jnp.log(1.0 + e))


def gelu(v):
    return jax.nn.gelu(v, approximate=True)


def rows_by_rows(values, weight):
    return lax.dot_general(
        values, weight, (((1,), (1,)), ((), ())), preferred_element_type=jnp.float32
    )


def load_blocks(blocks, place, pieces, weight, sems, first):
    copies = []
    for i, (piece, start, rows, slot) in enumerate(blocks):
        target = pl.multiple_of(place[slot] * rows, rows)
        copies.append(
            pltpu.make_async_copy(
                pieces[piece].at[pl.ds(start, rows), :],
                weight.at[pl.ds(target, rows), :],
                sems.at[first + i],
            )
        )
    for copy in copies:
        copy.start()
    return copies


def columns_of(j, step):
    return pl.ds(pl.multiple_of(j * step, step), step)


def own_features_kernel(step, values, weight, bias, out):
    product = jnp.dot(values[...], weight[...], preferred_element_type=jnp.float32)
    out[...] = gelu(product + bias[...]).astype(jnp.bfloat16)


def own_features(values, weight, bias):
    rows, width = values.shape
    step = 256
    return pl.pallas_call(
        functools.partial(own_features_kernel, step),
        grid=(width // step,),
        in_specs=[
            pl.BlockSpec((rows, width), lambda j: (0, 0)),
            pl.BlockSpec((width, step), lambda j: (0, j)),
            pl.BlockSpec((1, step), lambda j: (0, j)),
        ],
        out_specs=pl.BlockSpec((rows, step), lambda j: (0, j)),
        out_shape=jax.ShapeDtypeStruct((rows, width), jnp.bfloat16),
        compiler_params=params(),
        cost_estimate=cost(2 * rows * width * width, 2 * width * width),
        name="own_features",
    )(values, weight, bias)


def own_near_kernel(blocks, step, place, values, bias, *rest):
    *pieces, out, weight, sems = rest
    for copy in load_blocks(blocks, place, pieces, weight, sems, 0):
        copy.wait()

    @pl.loop(0, out.shape[1] // step)
    def _(j):
        columns = columns_of(j, step)
        product = rows_by_rows(values[...], weight[columns, :])
        out[:, columns] = softplus(product + bias[:, columns]).astype(jnp.bfloat16)


def own_near(values, bias, pieces, blocks, place):
    rows, width = values.shape
    tracks = bias.shape[1]
    vmem = pl.BlockSpec(memory_space=pltpu.VMEM)
    return pl.pallas_call(
        functools.partial(own_near_kernel, blocks, 384),
        in_specs=[pl.BlockSpec(memory_space=pltpu.SMEM), vmem, vmem]
        + [pl.BlockSpec(memory_space=pl.ANY)] * len(pieces),
        out_specs=vmem,
        out_shape=jax.ShapeDtypeStruct((rows, tracks), jnp.bfloat16),
        scratch_shapes=[
            pltpu.VMEM((tracks, width), jnp.bfloat16),
            pltpu.SemaphoreType.DMA((len(blocks),)),
        ],
        compiler_params=params(),
        cost_estimate=cost(2 * rows * width * tracks, 2 * width * tracks),
        name="own_near",
    )(place, values, bias, *pieces)


def finish_kernel(
    near_blocks,
    far_blocks,
    place,
    own_values,
    other_values,
    own_near_heads,
    sep_bias,
    head_bias,
    pair,
    sep_weight,
    *rest,
):
    bins, width = own_values.shape
    tracks = head_bias.shape[1]
    half_tracks = tracks // 2
    count = 1 + max(piece for piece, *_ in near_blocks)
    near_pieces, far_pieces = rest[:count], rest[count : 2 * count]
    out, sep, near, far, values, own, other, chosen, result, sems = rest[2 * count :]
    sep_copy = pltpu.make_async_copy(sep_weight, sep, sems.at[0])
    sep_copy.start()
    near_copies = load_blocks(near_blocks, place, near_pieces, near, sems, 1)
    far_copies = load_blocks(far_blocks, place, far_pieces, far, sems, 1 + len(near_blocks))
    which = place[place.shape[0] - 1]
    near_start = which * half_tracks
    far_start = (1 - which) * half_tracks

    values[:bins, :] = own_values[...]
    sep_copy.wait()

    @pl.loop(0, width // 256)
    def _(j):
        columns = columns_of(j, 256)
        product = jnp.dot(
            other_values[...], sep[:, columns], preferred_element_type=jnp.float32
        )
        values[bins:, columns] = gelu(product + sep_bias[:, columns]).astype(jnp.bfloat16)

    step = 384
    for copy in near_copies:
        copy.wait()

    @pl.loop(0, half_tracks // step)
    def _(j):
        columns = columns_of(j, step)
        target = pl.ds(pl.multiple_of(near_start + j * step, 128), step)
        product = rows_by_rows(values[bins:, :], near[columns, :])
        other[:, target] = softplus(product + head_bias[:, target]).astype(jnp.bfloat16)
        own[:, target] = own_near_heads[:, columns]

    for copy in far_copies:
        copy.wait()

    @pl.loop(0, half_tracks // step)
    def _(j):
        columns = columns_of(j, step)
        target = pl.ds(pl.multiple_of(far_start + j * step, 128), step)
        product = rows_by_rows(values[...], far[columns, :])
        heads = softplus(product + head_bias[:, target]).astype(jnp.bfloat16)
        own[:, target] = heads[:bins]
        other[:, target] = heads[bins:]

    step = 256

    def choose(j, slot):
        rows = lax.broadcasted_iota(jnp.int32, (tracks, step), 0)
        hit = rows == pair[:, columns_of(j, step)]
        chosen[slot] = jnp.where(hit, 1.0, 0.0).astype(jnp.bfloat16)

    def result_copy(j):
        columns = columns_of(j, step)
        return pltpu.make_async_copy(
            result.at[:, columns], out.at[:, columns], sems.at[sems.shape[0] - 1]
        )

    def combine(j, slot):
        columns = columns_of(j, step)
        received = jnp.dot(other[...], chosen[slot], preferred_element_type=jnp.float32)
        average = 0.5 * (own[:, columns].astype(jnp.float32) + received)
        result[:, columns] = average.astype(jnp.bfloat16)

    last = tracks // step - 1
    choose(0, 0)

    @pl.loop(0, last // 2)
    def _(i):
        combine(2 * i, 0)
        choose(2 * i + 1, 1)
        combine(2 * i + 1, 1)
        choose(2 * i + 2, 0)

    if last % 2:
        combine(last - 1, 0)
        choose(last, 1)
    combine(last, last % 2)
    done = pltpu.make_async_copy(result, out, sems.at[sems.shape[0] - 1])
    done.start()
    done.wait()


def finish(
    place, own_values, other_values, own_near_heads, sep_bias, head_bias, pair, sep_weight,
    near_pieces, far_pieces, near_blocks, far_blocks,
):
    bins, width = own_values.shape
    tracks = head_bias.shape[1]
    vmem = pl.BlockSpec(memory_space=pltpu.VMEM)
    anywhere = pl.BlockSpec(memory_space=pl.ANY)
    bf16 = lambda *shape: pltpu.VMEM(shape, jnp.bfloat16)
    return pl.pallas_call(
        functools.partial(finish_kernel, near_blocks, far_blocks),
        in_specs=[pl.BlockSpec(memory_space=pltpu.SMEM)]
        + [vmem] * 6
        + [anywhere] * (1 + len(near_pieces) + len(far_pieces)),
        out_specs=anywhere,
        out_shape=jax.ShapeDtypeStruct((bins, tracks), jnp.bfloat16),
        scratch_shapes=[
            bf16(width, width),
            bf16(tracks // 2, width),
            bf16(tracks // 2, width),
            bf16(2 * bins, width),
            bf16(bins, tracks),
            bf16(bins, tracks),
            bf16(2, tracks, 256),
            bf16(bins, tracks),
            pltpu.SemaphoreType.DMA((2 + len(near_blocks) + len(far_blocks),)),
        ],
        compiler_params=params(),
        cost_estimate=cost(8 * bins * tracks * tracks, 16 * bins * tracks),
        name="finish",
    )(
        place, own_values, other_values, own_near_heads, sep_bias, head_bias, pair, sep_weight,
        *near_pieces, *far_pieces,
    )


def along_line(s, b):
    return s ^ 4, b


def across_middle(s, b):
    return ((3 - s // 4) * 4 + s % 4, b) if s // 4 in (1, 2) else None


def to_line_ends(s, b):
    return (s ^ 4, b) if s // 4 in (1, 2) else None


def across_pair(s, b):
    return s ^ 2, b


def across_cores(s, b):
    return s ^ 1, b


def blocks_of(rows, first):
    blocks = []
    for group in range(2):
        base, slot = 3 * group, first + 4 * group
        blocks += [(base, 0, rows, slot), (base + 1, 0, rows, slot + 1)]
        blocks += [(base + 2, 0, rows, slot + 2), (base + 2, rows, rows, slot + 3)]
    return blocks


def places():
    s = lax.axis_index("seq")
    z, y, c = s // 4, (s // 2) % 2, s % 2
    inner = jnp.where(z < 2, 2, 1)
    result = []
    for zz in (z, z ^ 1, inner, inner ^ 1):
        for core in (c, 1 - c):
            for yy in (y, 1 - y):
                result.append((zz % 2) * 4 + yy * 2 + core)
    return jnp.stack(result + [s // 8]).astype(jnp.int32)


def edge(coarse_row, skip_row):
    total = coarse_row.astype(jnp.float32) + skip_row.astype(jnp.float32)
    return total.astype(jnp.bfloat16)


def tied(*trees):
    return lax.optimization_barrier(trees)


def per_device_tree(
    coarse, skip, depth_kernel, sep_weight, sep_bias, head_weight, head_bias, strand_pair
):
    seq, batch = lax.axis_size("seq"), lax.axis_size("batch")
    coarse, skip = coarse[0], skip[0]
    bins = skip.shape[0]
    sep = gather_rows(sep_weight)
    first = edge(coarse[:1], skip[:1])
    last = edge(coarse[-1:], skip[-1:])
    top = send(last, lambda s, b: (s + 1, b) if s + 1 < seq else None)
    bottom = send(first, lambda s, b: (s - 1, b) if s > 0 else None)
    to_mirror = lambda s, b: (seq - 1 - s, (b + batch // 2) % batch)
    z = lax.axis_index("seq") // 4
    pick = lambda a, c: jnp.where((z == 1) | (z == 2), a, c)
    pair_of = lambda a, c: jnp.concatenate([a, c])

    own = head_weight.T
    near = send(own, along_line)
    q0 = send(own, across_middle)
    y0 = send(own, across_pair)
    own_values, flipped = conv(coarse, skip, top, bottom, depth_kernel)
    near, q0, y0, flipped = tied(near, q0, y0, flipped)

    q1 = send(near, across_middle)
    y1 = send(near, across_pair)
    s0 = send(q0, to_line_ends)
    c0 = send(pair_of(own, y0), across_cores)
    q1, y1, s0, c0, flipped = tied(q1, y1, s0, c0, flipped)

    m0 = send(flipped[: bins // 2], to_mirror)
    o0 = pick(q0, s0)
    y2 = send(o0, across_pair)
    s1 = send(q1, to_line_ends)
    c1 = send(pair_of(near, y1), across_cores)
    m0, y2, s1, c1, sep, flipped = tied(m0, y2, s1, c1, sep, flipped)

    m1 = send(flipped[bins // 2 :], to_mirror)
    o1 = pick(q1, s1)
    y3 = send(o1, across_pair)
    c2 = send(pair_of(o0, y2), across_cores)
    place = places()
    rows = own.shape[0]
    values = own_features(own_values, sep, sep_bias[None])
    near_pieces = [own, y0, c0, near, y1, c1]
    half = place[-1]
    bias = lax.dynamic_slice_in_dim(
        head_bias[None], half * (head_bias.shape[0] // 2), head_bias.shape[0] // 2, axis=1
    )
    near_blocks = blocks_of(rows, 0)
    own_heads = own_near(values, bias, near_pieces, near_blocks, place)
    m1, y3, c2, own_heads = tied(m1, y3, c2, own_heads)

    c3 = send(pair_of(o1, y3), across_cores)
    return finish(
        place,
        values,
        jnp.concatenate([m0, m1]),
        own_heads,
        sep_bias[None],
        head_bias[None],
        strand_pair[None],
        sep,
        near_pieces,
        [o0, y2, c2, o1, y3, c3],
        near_blocks,
        blocks_of(rows, 8),
    )[None]


def plain_features_kernel(own, other, weight, bias, out):
    bins = own.shape[0]
    for place, part in enumerate((own, other)):
        product = jnp.dot(part[...], weight[...], preferred_element_type=jnp.float32)
        out[pl.ds(place * bins, bins), :] = jax.nn.gelu(
            product + bias[...], approximate=True
        ).astype(jnp.bfloat16)


def plain_features(own, other, weight, bias):
    bins, width = own.shape
    step = 256
    whole = pl.BlockSpec((bins, width), lambda j: (0, 0))
    return pl.pallas_call(
        plain_features_kernel,
        grid=(width // step,),
        in_specs=[
            whole,
            whole,
            pl.BlockSpec((width, step), lambda j: (0, j)),
            pl.BlockSpec((1, step), lambda j: (0, j)),
        ],
        out_specs=pl.BlockSpec((2 * bins, step), lambda j: (0, j)),
        out_shape=jax.ShapeDtypeStruct((2 * bins, width), jnp.bfloat16),
        compiler_params=params(),
        name="features",
    )(own, other, weight, bias)


def plain_heads_kernel(values, weight, bias, out):
    product = lax.dot_general(
        values[...], weight[...], (((1,), (1,)), ((), ())), preferred_element_type=jnp.float32
    )
    out[...] = softplus(product + bias[...]).astype(jnp.bfloat16)


def plain_heads(values, weight, bias):
    rows, width = values.shape
    tracks = weight.shape[0]
    step = 256
    return pl.pallas_call(
        plain_heads_kernel,
        grid=(tracks // step,),
        in_specs=[
            pl.BlockSpec((rows, width), lambda j: (0, 0)),
            pl.BlockSpec((step, width), lambda j: (j, 0)),
            pl.BlockSpec((1, step), lambda j: (0, j)),
        ],
        out_specs=pl.BlockSpec((rows, step), lambda j: (0, j)),
        out_shape=jax.ShapeDtypeStruct((rows, tracks), jnp.bfloat16),
        compiler_params=params(),
        name="heads",
    )(values, weight, bias)


def plain_average_kernel(own, other, pair, out):
    tracks = other.shape[1]
    rows = lax.broadcasted_iota(jnp.int32, (tracks, pair.shape[1]), 0)
    chosen = jnp.where(rows == pair[...], 1.0, 0.0).astype(jnp.bfloat16)
    received = jnp.dot(other[...], chosen, preferred_element_type=jnp.float32)
    out[...] = (0.5 * (own[...].astype(jnp.float32) + received)).astype(jnp.bfloat16)


def plain_average(both, pair):
    rows, tracks = both.shape
    bins = rows // 2
    step = 256
    return pl.pallas_call(
        plain_average_kernel,
        grid=(tracks // step,),
        in_specs=[
            pl.BlockSpec((bins, step), lambda j: (0, j)),
            pl.BlockSpec((bins, tracks), lambda j: (1, 0)),
            pl.BlockSpec((1, step), lambda j: (0, j)),
        ],
        out_specs=pl.BlockSpec((bins, step), lambda j: (0, j)),
        out_shape=jax.ShapeDtypeStruct((bins, tracks), jnp.bfloat16),
        compiler_params=params(),
        name="average",
    )(both, both, pair)


def gather_rows(shard):
    batch = lax.axis_size("batch")
    part = shard.shape[0] // batch
    mine = lax.dynamic_slice_in_dim(shard, lax.axis_index("batch") * part, part, axis=0)
    return lax.all_gather(mine, BOTH, axis=0, tiled=True)


def per_device_plain(
    coarse, skip, depth_kernel, sep_weight, sep_bias, head_weight, head_bias, strand_pair
):
    seq, batch = lax.axis_size("seq"), lax.axis_size("batch")
    coarse, skip = coarse[0], skip[0]
    first = edge(coarse[:1], skip[:1])
    last = edge(coarse[-1:], skip[-1:])
    top = send(last, lambda s, b: (s + 1, b) if s + 1 < seq else None)
    bottom = send(first, lambda s, b: (s - 1, b) if s > 0 else None)
    own, flipped = conv(coarse, skip, top, bottom, depth_kernel)
    other = send(flipped, lambda s, b: (seq - 1 - s, (b + batch // 2) % batch))
    values = plain_features(own, other, gather_rows(sep_weight), sep_bias[None])
    both = plain_heads(values, gather_rows(head_weight.T), head_bias[None])
    return plain_average(both, strand_pair[None])[None]


def solution(mesh):
    tree = mesh.shape["seq"] == 16 and mesh.shape["batch"] == 2
    in_specs = (
        P("batch", "seq", None),
        P("batch", "seq", None),
        P(),
        P("seq", None),
        P(),
        P(None, "seq"),
        P(),
        P(),
    )
    out_specs = P("batch", "seq", None)
    return jax.shard_map(
        per_device_tree if tree else per_device_plain,
        mesh=mesh,
        in_specs=in_specs,
        out_specs=out_specs,
        check_vma=False,
    )
```

```python
import functools

import jax
import jax.numpy as jnp
from jax import lax
from jax.experimental import pallas as pl
from jax.experimental.pallas import tpu as pltpu
from jax.sharding import PartitionSpec as P

BOTH = ("seq", "batch")
VMEM_LIMIT = 56 * 1024 * 1024


def params():
    return pltpu.CompilerParams(vmem_limit_bytes=VMEM_LIMIT)


def cost(flops, bytes_accessed):
    return pl.CostEstimate(flops=flops, bytes_accessed=bytes_accessed, transcendentals=0)


def route(seq, batch, move):
    pairs = []
    for s in range(seq):
        for b in range(batch):
            target = move(s, b)
            if target is not None:
                pairs.append((s * batch + b, target[0] * batch + target[1]))
    return pairs


def send(array, move):
    seq, batch = lax.axis_size("seq"), lax.axis_size("batch")
    return lax.ppermute(array, BOTH, route(seq, batch, move))


def one_hot(shape, hit):
    rows = lax.broadcasted_iota(jnp.int32, shape, 0)
    columns = lax.broadcasted_iota(jnp.int32, shape, 1)
    return jnp.where(hit(rows, columns), 1.0, 0.0).astype(jnp.bfloat16)


def conv_kernel(coarse, skip, top, bottom, taps, own, *flipped):
    bins = skip.shape[0]
    spread = one_hot((bins, coarse.shape[0]), lambda r, c: r // 2 == c)
    up = jnp.dot(spread, coarse[...], preferred_element_type=jnp.float32)
    merged = (up + skip[...].astype(jnp.float32)).astype(jnp.bfloat16).astype(jnp.float32)
    row = lax.broadcasted_iota(jnp.int32, merged.shape, 0)
    before = jnp.where(row == 0, top[...].astype(jnp.float32), pltpu.roll(merged, 1, 0))
    after = jnp.where(
        row == bins - 1, bottom[...].astype(jnp.float32), pltpu.roll(merged, bins - 1, 0)
    )
    result = taps[0:1, :] * before + taps[1:2, :] * merged + taps[2:3, :] * after
    result = result.astype(jnp.bfloat16)
    own[...] = result
    mirror = one_hot((bins, bins), lambda r, c: r + c == bins - 1)
    turned = jnp.dot(mirror, result, preferred_element_type=jnp.float32).astype(jnp.bfloat16)
    start = 0
    for part in flipped:
        part[...] = turned[start : start + part.shape[0]]
        start += part.shape[0]


def conv(coarse, skip, top, bottom, taps, cut=()):
    bins, width = skip.shape
    step = 256
    parts = [b - a for a, b in zip((0, *cut), (*cut, bins))]
    column = lambda rows: pl.BlockSpec((rows, step), lambda j: (0, j))
    return pl.pallas_call(
        conv_kernel,
        grid=(width // step,),
        in_specs=[column(coarse.shape[0]), column(bins), column(1), column(1), column(3)],
        out_specs=[column(rows) for rows in (bins, *parts)],
        out_shape=[jax.ShapeDtypeStruct((rows, width), jnp.bfloat16) for rows in (bins, *parts)],
        compiler_params=params(),
        cost_estimate=cost(2 * bins * bins * width, 6 * bins * width),
        name="conv",
    )(coarse, skip, top, bottom, taps)


def softplus(v):
    e = jnp.exp(-jnp.abs(v))
    return jnp.maximum(v, 0.0) + jnp.where(e < 1e-4, e, jnp.log(1.0 + e))


def gelu(v):
    return jax.nn.gelu(v, approximate=True)


def rows_by_rows(values, weight):
    return lax.dot_general(
        values, weight, (((1,), (1,)), ((), ())), preferred_element_type=jnp.float32
    )


def columns_of(j, step):
    return pl.ds(pl.multiple_of(j * step, step), step)


def finish_kernel(place, sep_bias, head_bias, pair, own_values, *rest):
    shards = place.shape[0]
    parts = len(rest) - shards - 10
    others, pieces = rest[:parts], rest[parts : parts + shards]
    out, sep, head, inputs, values, own, other, chosen, result, sems = rest[parts + shards :]
    bins, tracks = own.shape
    width = values.shape[1]
    depth = width // shards
    share = tracks // shards
    copies = []

    def fetch(source, target):
        copy = pltpu.make_async_copy(source, target, sems.at[len(copies)])
        copy.start()
        copies.append(copy)

    fetch(own_values, inputs.at[pl.ds(0, bins), :])
    start = bins
    for part in others:
        fetch(part, inputs.at[pl.ds(start, part.shape[0]), :])
        start += part.shape[0]
    for i, piece in enumerate(pieces):
        target = pl.multiple_of(place[i] * depth, depth)
        fetch(piece.at[pl.ds(0, depth), :], sep.at[pl.ds(target, depth), :])
    first = len(copies)
    for i, piece in enumerate(pieces):
        target = pl.multiple_of(place[i] * share, share)
        fetch(piece.at[pl.ds(depth, share), :], head.at[pl.ds(target, share), :])
    for copy in copies[:first]:
        copy.wait()

    @pl.loop(0, width // 256)
    def _(j):
        columns = columns_of(j, 256)
        product = jnp.dot(inputs[...], sep[:, columns], preferred_element_type=jnp.float32)
        values[:, columns] = gelu(product + sep_bias[:, columns]).astype(jnp.bfloat16)

    for copy in copies[first:]:
        copy.wait()
    step = 256

    @pl.loop(0, tracks // step)
    def _(j):
        columns = columns_of(j, step)
        product = rows_by_rows(values[...], head[columns, :])
        heads = softplus(product + head_bias[:, columns]).astype(jnp.bfloat16)
        own[:, columns] = heads[:bins]
        other[:, columns] = heads[bins:]

    used = len(copies)

    def choose(j, slot):
        rows = lax.broadcasted_iota(jnp.int32, (tracks, step), 0)
        hit = rows == pair[:, columns_of(j, step)]
        chosen[slot] = jnp.where(hit, 1.0, 0.0).astype(jnp.bfloat16)

    def result_copy(j):
        columns = columns_of(j, step)
        return pltpu.make_async_copy(
            result.at[:, columns], out.at[:, columns], sems.at[used + j]
        )

    def combine(j, slot):
        columns = columns_of(j, step)
        received = jnp.dot(other[...], chosen[slot], preferred_element_type=jnp.float32)
        average = 0.5 * (own[:, columns].astype(jnp.float32) + received)
        result[:, columns] = average.astype(jnp.bfloat16)
        result_copy(j).start()

    last = tracks // step - 1
    choose(0, 0)

    @pl.loop(0, last // 2)
    def _(i):
        combine(2 * i, 0)
        choose(2 * i + 1, 1)
        combine(2 * i + 1, 1)
        choose(2 * i + 2, 0)

    if last % 2:
        combine(last - 1, 0)
        choose(last, 1)
    combine(last, last % 2)
    for j in range(last + 1):
        result_copy(j).wait()


def finish(place, sep_bias, head_bias, pair, own_values, others, pieces):
    bins, width = own_values.shape
    tracks = head_bias.shape[1]
    vmem = pl.BlockSpec(memory_space=pltpu.VMEM)
    anywhere = pl.BlockSpec(memory_space=pl.ANY)
    bf16 = lambda *shape: pltpu.VMEM(shape, jnp.bfloat16)
    count = 1 + len(others) + 2 * len(pieces) + tracks // 256
    return pl.pallas_call(
        finish_kernel,
        in_specs=[pl.BlockSpec(memory_space=pltpu.SMEM)]
        + [vmem] * 3
        + [anywhere] * (1 + len(others) + len(pieces)),
        out_specs=anywhere,
        out_shape=jax.ShapeDtypeStruct((bins, tracks), jnp.bfloat16),
        scratch_shapes=[
            bf16(width, width),
            bf16(tracks, width),
            bf16(2 * bins, width),
            bf16(2 * bins, width),
            bf16(bins, tracks),
            bf16(bins, tracks),
            bf16(2, tracks, 256),
            bf16(bins, tracks),
            pltpu.SemaphoreType.DMA((count,)),
        ],
        compiler_params=params(),
        cost_estimate=cost(8 * bins * tracks * tracks, 16 * bins * tracks),
        name="finish",
    )(place, sep_bias, head_bias, pair, own_values, *others, *pieces)


def along_line(s, b):
    return s ^ 4, b


def across_middle(s, b):
    return ((3 - s // 4) * 4 + s % 4, b) if s // 4 in (1, 2) else None


def to_line_ends(s, b):
    return (s ^ 4, b) if s // 4 in (1, 2) else None


def across_pair(s, b):
    return s ^ 2, b


def across_cores(s, b):
    return s ^ 1, b


def places():
    s = lax.axis_index("seq")
    z, y, c = s // 4, (s // 2) % 2, s % 2
    inner = jnp.where(z < 2, 2, 1)
    result = []
    for zz in (z, z ^ 1, inner, inner ^ 1):
        for core in (c, 1 - c):
            for yy in (y, 1 - y):
                result.append(zz * 4 + yy * 2 + core)
    return jnp.stack(result).astype(jnp.int32)


def edge(coarse_row, skip_row):
    total = coarse_row.astype(jnp.float32) + skip_row.astype(jnp.float32)
    return total.astype(jnp.bfloat16)


def tied(*trees):
    return lax.optimization_barrier(trees)


def per_device_tree(
    coarse, skip, depth_kernel, sep_weight, sep_bias, head_weight, head_bias, strand_pair
):
    seq, batch = lax.axis_size("seq"), lax.axis_size("batch")
    coarse, skip = coarse[0], skip[0]
    first = edge(coarse[:1], skip[:1])
    last = edge(coarse[-1:], skip[-1:])
    top = send(last, lambda s, b: (s + 1, b) if s + 1 < seq else None)
    bottom = send(first, lambda s, b: (s - 1, b) if s > 0 else None)
    to_mirror = lambda s, b: (seq - 1 - s, (b + batch // 2) % batch)
    z = lax.axis_index("seq") // 4
    pick = lambda a, c: jnp.where((z == 1) | (z == 2), a, c)

    own = jnp.concatenate([sep_weight, head_weight.T])
    near = send(own, along_line)
    q0 = send(own, across_middle)
    y0 = send(own, across_pair)
    k_own = send(own, across_cores)
    small = (sep_bias[None], head_bias[None], strand_pair[None], places())
    edges = (top, bottom)
    near, q0, y0, k_own, edges, small = tied(near, q0, y0, k_own, edges, small)
    sep_bias, head_bias, strand_pair, place = small

    top, bottom = edges
    own_values, *flipped = conv(coarse, skip, top, bottom, depth_kernel, (skip.shape[0] // 2,))
    q1 = send(near, across_middle)
    y1 = send(near, across_pair)
    s0 = send(q0, to_line_ends)
    k_y0 = send(y0, across_cores)
    k_near = send(near, across_cores)
    q1, y1, s0, k_y0, k_near, flipped, own_values = tied(
        q1, y1, s0, k_y0, k_near, flipped, own_values
    )

    m0 = send(flipped[0], to_mirror)
    o0 = pick(q0, s0)
    y2 = send(o0, across_pair)
    s1 = send(q1, to_line_ends)
    k_y1 = send(y1, across_cores)
    k_o0 = send(o0, across_cores)
    m0, y2, s1, k_y1, k_o0, flipped = tied(m0, y2, s1, k_y1, k_o0, flipped)

    m1 = send(flipped[1], to_mirror)
    o1 = pick(q1, s1)
    y3 = send(o1, across_pair)
    k_y2 = send(y2, across_cores)
    k_o1 = send(o1, across_cores)
    m1, y3, k_y2, k_o1 = tied(m1, y3, k_y2, k_o1)

    k_y3 = send(y3, across_cores)
    pieces = [own, y0, k_own, k_y0, near, y1, k_near, k_y1]
    pieces += [o0, y2, k_o0, k_y2, o1, y3, k_o1, k_y3]
    return finish(place, sep_bias, head_bias, strand_pair, own_values, [m0, m1], pieces)[None]


def plain_features_kernel(own, other, weight, bias, out):
    bins = own.shape[0]
    for place, part in enumerate((own, other)):
        product = jnp.dot(part[...], weight[...], preferred_element_type=jnp.float32)
        out[pl.ds(place * bins, bins), :] = jax.nn.gelu(
            product + bias[...], approximate=True
        ).astype(jnp.bfloat16)


def plain_features(own, other, weight, bias):
    bins, width = own.shape
    step = 256
    whole = pl.BlockSpec((bins, width), lambda j: (0, 0))
    return pl.pallas_call(
        plain_features_kernel,
        grid=(width // step,),
        in_specs=[
            whole,
            whole,
            pl.BlockSpec((width, step), lambda j: (0, j)),
            pl.BlockSpec((1, step), lambda j: (0, j)),
        ],
        out_specs=pl.BlockSpec((2 * bins, step), lambda j: (0, j)),
        out_shape=jax.ShapeDtypeStruct((2 * bins, width), jnp.bfloat16),
        compiler_params=params(),
        name="features",
    )(own, other, weight, bias)


def plain_heads_kernel(values, weight, bias, out):
    product = lax.dot_general(
        values[...], weight[...], (((1,), (1,)), ((), ())), preferred_element_type=jnp.float32
    )
    out[...] = softplus(product + bias[...]).astype(jnp.bfloat16)


def plain_heads(values, weight, bias):
    rows, width = values.shape
    tracks = weight.shape[0]
    step = 256
    return pl.pallas_call(
        plain_heads_kernel,
        grid=(tracks // step,),
        in_specs=[
            pl.BlockSpec((rows, width), lambda j: (0, 0)),
            pl.BlockSpec((step, width), lambda j: (j, 0)),
            pl.BlockSpec((1, step), lambda j: (0, j)),
        ],
        out_specs=pl.BlockSpec((rows, step), lambda j: (0, j)),
        out_shape=jax.ShapeDtypeStruct((rows, tracks), jnp.bfloat16),
        compiler_params=params(),
        name="heads",
    )(values, weight, bias)


def plain_average_kernel(own, other, pair, out):
    tracks = other.shape[1]
    rows = lax.broadcasted_iota(jnp.int32, (tracks, pair.shape[1]), 0)
    chosen = jnp.where(rows == pair[...], 1.0, 0.0).astype(jnp.bfloat16)
    received = jnp.dot(other[...], chosen, preferred_element_type=jnp.float32)
    out[...] = (0.5 * (own[...].astype(jnp.float32) + received)).astype(jnp.bfloat16)


def plain_average(both, pair):
    rows, tracks = both.shape
    bins = rows // 2
    step = 256
    return pl.pallas_call(
        plain_average_kernel,
        grid=(tracks // step,),
        in_specs=[
            pl.BlockSpec((bins, step), lambda j: (0, j)),
            pl.BlockSpec((bins, tracks), lambda j: (1, 0)),
            pl.BlockSpec((1, step), lambda j: (0, j)),
        ],
        out_specs=pl.BlockSpec((bins, step), lambda j: (0, j)),
        out_shape=jax.ShapeDtypeStruct((bins, tracks), jnp.bfloat16),
        compiler_params=params(),
        name="average",
    )(both, both, pair)


def gather_rows(shard):
    batch = lax.axis_size("batch")
    part = shard.shape[0] // batch
    mine = lax.dynamic_slice_in_dim(shard, lax.axis_index("batch") * part, part, axis=0)
    return lax.all_gather(mine, BOTH, axis=0, tiled=True)


def per_device_plain(
    coarse, skip, depth_kernel, sep_weight, sep_bias, head_weight, head_bias, strand_pair
):
    seq, batch = lax.axis_size("seq"), lax.axis_size("batch")
    coarse, skip = coarse[0], skip[0]
    first = edge(coarse[:1], skip[:1])
    last = edge(coarse[-1:], skip[-1:])
    top = send(last, lambda s, b: (s + 1, b) if s + 1 < seq else None)
    bottom = send(first, lambda s, b: (s - 1, b) if s > 0 else None)
    own, flipped = conv(coarse, skip, top, bottom, depth_kernel)
    other = send(flipped, lambda s, b: (seq - 1 - s, (b + batch // 2) % batch))
    values = plain_features(own, other, gather_rows(sep_weight), sep_bias[None])
    both = plain_heads(values, gather_rows(head_weight.T), head_bias[None])
    return plain_average(both, strand_pair[None])[None]


def solution(mesh):
    tree = mesh.shape["seq"] == 16 and mesh.shape["batch"] == 2
    in_specs = (
        P("batch", "seq", None),
        P("batch", "seq", None),
        P(),
        P("seq", None),
        P(),
        P(None, "seq"),
        P(),
        P(),
    )
    out_specs = P("batch", "seq", None)
    return jax.shard_map(
        per_device_tree if tree else per_device_plain,
        mesh=mesh,
        in_specs=in_specs,
        out_specs=out_specs,
        check_vma=False,
    )
```

```python
import functools

import jax
import jax.numpy as jnp
from jax import lax
from jax.experimental import pallas as pl
from jax.experimental.pallas import tpu as pltpu
from jax.sharding import PartitionSpec as P

BOTH = ("seq", "batch")
VMEM_LIMIT = 56 * 1024 * 1024


def params():
    return pltpu.CompilerParams(vmem_limit_bytes=VMEM_LIMIT)


def cost(flops, bytes_accessed):
    return pl.CostEstimate(flops=flops, bytes_accessed=bytes_accessed, transcendentals=0)


def route(seq, batch, move):
    pairs = []
    for s in range(seq):
        for b in range(batch):
            target = move(s, b)
            if target is not None:
                pairs.append((s * batch + b, target[0] * batch + target[1]))
    return pairs


def send(array, move):
    seq, batch = lax.axis_size("seq"), lax.axis_size("batch")
    return lax.ppermute(array, BOTH, route(seq, batch, move))


def one_hot(shape, hit):
    rows = lax.broadcasted_iota(jnp.int32, shape, 0)
    columns = lax.broadcasted_iota(jnp.int32, shape, 1)
    return jnp.where(hit(rows, columns), 1.0, 0.0).astype(jnp.bfloat16)


def conv_kernel(coarse, skip, top, bottom, taps, own, *flipped):
    bins = skip.shape[0]
    spread = one_hot((bins, coarse.shape[0]), lambda r, c: r // 2 == c)
    up = jnp.dot(spread, coarse[...], preferred_element_type=jnp.float32)
    merged = (up + skip[...].astype(jnp.float32)).astype(jnp.bfloat16).astype(jnp.float32)
    row = lax.broadcasted_iota(jnp.int32, merged.shape, 0)
    before = jnp.where(row == 0, top[...].astype(jnp.float32), pltpu.roll(merged, 1, 0))
    after = jnp.where(
        row == bins - 1, bottom[...].astype(jnp.float32), pltpu.roll(merged, bins - 1, 0)
    )
    result = taps[0:1, :] * before + taps[1:2, :] * merged + taps[2:3, :] * after
    result = result.astype(jnp.bfloat16)
    own[...] = result
    mirror = one_hot((bins, bins), lambda r, c: r + c == bins - 1)
    turned = jnp.dot(mirror, result, preferred_element_type=jnp.float32).astype(jnp.bfloat16)
    start = 0
    for part in flipped:
        part[...] = turned[start : start + part.shape[0]]
        start += part.shape[0]


def conv(coarse, skip, top, bottom, taps, cut=()):
    bins, width = skip.shape
    step = 256
    parts = [b - a for a, b in zip((0, *cut), (*cut, bins))]
    column = lambda rows: pl.BlockSpec((rows, step), lambda j: (0, j))
    return pl.pallas_call(
        conv_kernel,
        grid=(width // step,),
        in_specs=[column(coarse.shape[0]), column(bins), column(1), column(1), column(3)],
        out_specs=[column(rows) for rows in (bins, *parts)],
        out_shape=[jax.ShapeDtypeStruct((rows, width), jnp.bfloat16) for rows in (bins, *parts)],
        compiler_params=params(),
        cost_estimate=cost(2 * bins * bins * width, 6 * bins * width),
        name="conv",
    )(coarse, skip, top, bottom, taps)


def softplus(v):
    e = jnp.exp(-jnp.abs(v))
    return jnp.maximum(v, 0.0) + jnp.where(e < 1e-4, e, jnp.log(1.0 + e))


def gelu(v):
    return jax.nn.gelu(v, approximate=True)


def rows_by_rows(values, weight):
    return lax.dot_general(
        values, weight, (((1,), (1,)), ((), ())), preferred_element_type=jnp.float32
    )


def copies_of(blocks, place, pieces, weight, sems, first):
    copies = []
    for i, (piece, start, rows, slot) in enumerate(blocks):
        target = pl.multiple_of(place[slot] * rows, rows)
        copies.append(
            pltpu.make_async_copy(
                pieces[piece].at[pl.ds(start, rows), :],
                weight.at[pl.ds(target, rows), :],
                sems.at[first + i],
            )
        )
    return copies


def columns_of(j, step):
    return pl.ds(pl.multiple_of(j * step, step), step)


def early_kernel(sep_blocks, near_blocks, place, sep_bias, head_bias, own_values, first, *rest):
    *pieces, values, heads, sep, near, inputs, sems = rest
    bins, part = own_values.shape[0], first.shape[0]
    width, half_tracks = values.shape[1], heads.shape[1]
    which = place[place.shape[0] - 1]
    near_start = pl.multiple_of(which * half_tracks, 128)
    copies = copies_of(sep_blocks, place, pieces, sep, sems, 0)
    near_copies = copies_of(near_blocks, place, pieces, near, sems, len(sep_blocks))
    base = len(sep_blocks) + len(near_blocks)
    copies.append(
        pltpu.make_async_copy(own_values, inputs.at[pl.ds(0, bins), :], sems.at[base])
    )
    copies.append(
        pltpu.make_async_copy(first, inputs.at[pl.ds(bins, part), :], sems.at[base + 1])
    )
    for copy in copies + near_copies:
        copy.start()
    for copy in copies:
        copy.wait()

    @pl.loop(0, width // 256)
    def _(j):
        columns = columns_of(j, 256)
        product = jnp.dot(inputs[...], sep[:, columns], preferred_element_type=jnp.float32)
        values[:, columns] = gelu(product + sep_bias[:, columns]).astype(jnp.bfloat16)

    for copy in near_copies:
        copy.wait()
    step = 384

    @pl.loop(0, half_tracks // step)
    def _(j):
        columns = columns_of(j, step)
        source = pl.ds(pl.multiple_of(near_start + j * step, 128), step)
        product = rows_by_rows(values[...], near[columns, :])
        heads[:, columns] = softplus(product + head_bias[:, source]).astype(jnp.bfloat16)


def early(place, sep_bias, head_bias, own_values, first, pieces, sep_blocks, near_blocks):
    rows, width = own_values.shape[0] + first.shape[0], own_values.shape[1]
    half_tracks = head_bias.shape[1] // 2
    vmem = pl.BlockSpec(memory_space=pltpu.VMEM)
    shapes = [(rows, width), (rows, half_tracks)]
    return pl.pallas_call(
        functools.partial(early_kernel, sep_blocks, near_blocks),
        in_specs=[pl.BlockSpec(memory_space=pltpu.SMEM)]
        + [vmem] * 2
        + [pl.BlockSpec(memory_space=pl.ANY)] * (2 + len(pieces)),
        out_specs=[vmem] * 2,
        out_shape=[jax.ShapeDtypeStruct(shape, jnp.bfloat16) for shape in shapes],
        scratch_shapes=[
            pltpu.VMEM((width, width), jnp.bfloat16),
            pltpu.VMEM((half_tracks, width), jnp.bfloat16),
            pltpu.VMEM((rows, width), jnp.bfloat16),
            pltpu.SemaphoreType.DMA((2 + len(sep_blocks) + len(near_blocks),)),
        ],
        compiler_params=params(),
        cost_estimate=cost(2 * rows * width * (width + half_tracks), 4 * width * width),
        name="early",
    )(place, sep_bias, head_bias, own_values, first, *pieces)


def finish_kernel(sep_blocks, near_blocks, far_blocks, place, sep_bias, head_bias, pair, *rest):
    early_values, later, near_heads, *pieces = rest[:-11]
    out, sep, near, far, last_values, values, own, other, chosen, result, sems = rest[-11:]
    bins, tracks = own.shape
    part = early_values.shape[0] - bins
    width = values.shape[1]
    half_tracks = tracks // 2
    which = place[place.shape[0] - 1]
    near_start = pl.multiple_of(which * half_tracks, 128)
    far_start = pl.multiple_of((1 - which) * half_tracks, 128)
    near_columns = pl.ds(near_start, half_tracks)
    near_first = len(sep_blocks)
    far_first = near_first + len(near_blocks)
    base = far_first + len(far_blocks)

    def fetch(source, target, number):
        copy = pltpu.make_async_copy(source, target, sems.at[base + number])
        copy.start()
        return copy

    later_copy = fetch(later, last_values, 0)
    sep_copies = copies_of(sep_blocks, place, pieces, sep, sems, 0)
    near_copies = copies_of(near_blocks, place, pieces, near, sems, near_first)
    far_copies = copies_of(far_blocks, place, pieces, far, sems, far_first)
    for copy in sep_copies + near_copies:
        copy.start()
    values_copy = fetch(early_values, values.at[pl.ds(0, bins + part), :], 1)
    for copy in far_copies:
        copy.start()
    own_near_copy = fetch(near_heads.at[pl.ds(0, bins), :], own.at[:, near_columns], 2)
    first_near_copy = fetch(
        near_heads.at[pl.ds(bins, part), :], other.at[pl.ds(0, part), near_columns], 3
    )
    later_copy.wait()
    for copy in sep_copies:
        copy.wait()

    @pl.loop(0, width // 256)
    def _(j):
        columns = columns_of(j, 256)
        product = jnp.dot(
            last_values[...], sep[:, columns], preferred_element_type=jnp.float32
        )
        values[bins + part :, columns] = gelu(product + sep_bias[:, columns]).astype(
            jnp.bfloat16
        )

    step = 384
    for copy in near_copies:
        copy.wait()

    @pl.loop(0, half_tracks // step)
    def _(j):
        columns = columns_of(j, step)
        target = pl.ds(pl.multiple_of(near_start + j * step, 128), step)
        product = rows_by_rows(values[bins + part :, :], near[columns, :])
        other[part:, target] = softplus(product + head_bias[:, target]).astype(jnp.bfloat16)

    values_copy.wait()
    for copy in far_copies:
        copy.wait()

    @pl.loop(0, half_tracks // step)
    def _(j):
        columns = columns_of(j, step)
        target = pl.ds(pl.multiple_of(far_start + j * step, 128), step)
        product = rows_by_rows(values[...], far[columns, :])
        heads = softplus(product + head_bias[:, target]).astype(jnp.bfloat16)
        own[:, target] = heads[:bins]
        other[:, target] = heads[bins:]

    own_near_copy.wait()
    first_near_copy.wait()
    step = 256

    def choose(j, slot):
        rows = lax.broadcasted_iota(jnp.int32, (tracks, step), 0)
        hit = rows == pair[:, columns_of(j, step)]
        chosen[slot] = jnp.where(hit, 1.0, 0.0).astype(jnp.bfloat16)

    def result_copy(j):
        columns = columns_of(j, step)
        return pltpu.make_async_copy(
            result.at[:, columns], out.at[:, columns], sems.at[base + 4 + j]
        )

    def combine(j, slot):
        columns = columns_of(j, step)
        received = jnp.dot(other[...], chosen[slot], preferred_element_type=jnp.float32)
        average = 0.5 * (own[:, columns].astype(jnp.float32) + received)
        result[:, columns] = average.astype(jnp.bfloat16)
        result_copy(j).start()

    last = tracks // step - 1
    choose(0, 0)

    @pl.loop(0, last // 2)
    def _(i):
        combine(2 * i, 0)
        choose(2 * i + 1, 1)
        combine(2 * i + 1, 1)
        choose(2 * i + 2, 0)

    if last % 2:
        combine(last - 1, 0)
        choose(last, 1)
    combine(last, last % 2)
    for j in range(last + 1):
        result_copy(j).wait()


def finish(place, sep_bias, head_bias, pair, arrays, pieces, sep_blocks, near_blocks, far_blocks):
    last, width = arrays[1].shape
    bins = (arrays[0].shape[0] + last) // 2
    tracks = head_bias.shape[1]
    vmem = pl.BlockSpec(memory_space=pltpu.VMEM)
    anywhere = pl.BlockSpec(memory_space=pl.ANY)
    bf16 = lambda *shape: pltpu.VMEM(shape, jnp.bfloat16)
    count = len(sep_blocks) + len(near_blocks) + len(far_blocks) + 4 + tracks // 256
    return pl.pallas_call(
        functools.partial(finish_kernel, sep_blocks, near_blocks, far_blocks),
        in_specs=[pl.BlockSpec(memory_space=pltpu.SMEM)]
        + [vmem] * 3
        + [anywhere] * (len(arrays) + len(pieces)),
        out_specs=anywhere,
        out_shape=jax.ShapeDtypeStruct((bins, tracks), jnp.bfloat16),
        scratch_shapes=[
            bf16(width, width),
            bf16(tracks // 2, width),
            bf16(tracks // 2, width),
            bf16(last, width),
            bf16(2 * bins, width),
            bf16(bins, tracks),
            bf16(bins, tracks),
            bf16(2, tracks, 256),
            bf16(bins, tracks),
            pltpu.SemaphoreType.DMA((count,)),
        ],
        compiler_params=params(),
        cost_estimate=cost(8 * bins * tracks * tracks, 16 * bins * tracks),
        name="finish",
    )(place, sep_bias, head_bias, pair, *arrays, *pieces)


def along_line(s, b):
    return s ^ 4, b


def across_middle(s, b):
    return ((3 - s // 4) * 4 + s % 4, b) if s // 4 in (1, 2) else None


def to_line_ends(s, b):
    return (s ^ 4, b) if s // 4 in (1, 2) else None


def across_pair(s, b):
    return s ^ 2, b


def across_cores(s, b):
    return s ^ 1, b


def blocks_of(rows, starts, first):
    return [(i, start, rows, first + i) for i, start in enumerate(starts)]


def places():
    s = lax.axis_index("seq")
    z, y, c = s // 4, (s // 2) % 2, s % 2
    inner = jnp.where(z < 2, 2, 1)
    within, among = [], []
    for zz in (z, z ^ 1, inner, inner ^ 1):
        for core in (c, 1 - c):
            for yy in (y, 1 - y):
                within.append((zz % 2) * 4 + yy * 2 + core)
                among.append(zz * 4 + yy * 2 + core)
    return jnp.stack(within + among + [s // 8]).astype(jnp.int32)


def edge(coarse_row, skip_row):
    total = coarse_row.astype(jnp.float32) + skip_row.astype(jnp.float32)
    return total.astype(jnp.bfloat16)


def tied(*trees):
    return lax.optimization_barrier(trees)


def per_device_tree(
    coarse, skip, depth_kernel, sep_weight, sep_bias, head_weight, head_bias, strand_pair
):
    seq, batch = lax.axis_size("seq"), lax.axis_size("batch")
    coarse, skip = coarse[0], skip[0]
    first = edge(coarse[:1], skip[:1])
    last = edge(coarse[-1:], skip[-1:])
    top = send(last, lambda s, b: (s + 1, b) if s + 1 < seq else None)
    bottom = send(first, lambda s, b: (s - 1, b) if s > 0 else None)
    to_mirror = lambda s, b: (seq - 1 - s, (b + batch // 2) % batch)
    z = lax.axis_index("seq") // 4
    pick = lambda a, c: jnp.where((z == 1) | (z == 2), a, c)

    own = jnp.concatenate([sep_weight, head_weight.T])
    near = send(own, along_line)
    q0 = send(own, across_middle)
    y0 = send(own, across_pair)
    k_own = send(own, across_cores)
    small = (sep_bias, head_bias, strand_pair, places())
    edges = (top, bottom)
    near, q0, y0, k_own, edges, small = tied(near, q0, y0, k_own, edges, small)
    sep_bias, head_bias, strand_pair, place = small

    top, bottom = edges
    own_values, *flipped = conv(coarse, skip, top, bottom, depth_kernel, (5 * skip.shape[0] // 8,))
    q1 = send(near, across_middle)
    y1 = send(near, across_pair)
    s0 = send(q0, to_line_ends)
    k_y0 = send(y0, across_cores)
    k_near = send(near, across_cores)
    small = (sep_bias[None], head_bias[None], strand_pair[None], place)
    q1, y1, s0, k_y0, k_near, flipped, own_values, small = tied(
        q1, y1, s0, k_y0, k_near, flipped, own_values, small
    )
    sep_bias, head_bias, strand_pair, place = small

    m0 = send(flipped[0], to_mirror)
    o0 = pick(q0, s0)
    y2 = send(o0, across_pair)
    s1 = send(q1, to_line_ends)
    k_y1 = send(y1, across_cores)
    k_o0 = send(o0, across_cores)
    m0, y2, s1, k_y1, k_o0, flipped = tied(m0, y2, s1, k_y1, k_o0, flipped)

    depth = sep_weight.shape[0]
    o1_sep, o1_head = pick(q1[:depth], s1[:depth]), pick(q1[depth:], s1[depth:])
    y3_sep = send(o1_sep, across_pair)
    k_y2 = send(y2, across_cores)
    k_o1_sep = send(o1_sep, across_cores)
    y3_sep, o1_head, last_part = tied(y3_sep, o1_head, flipped[1])

    m1 = send(last_part, to_mirror)
    y3 = send(o1_head, across_pair)
    k_y3_sep = send(y3_sep, across_cores)
    k_o1 = send(o1_head, across_cores)
    near_pieces = [own, y0, k_own, k_y0, near, y1, k_near, k_y1]
    far_pieces = [o0, y2, k_o0, k_y2]
    rows = own.shape[0] - depth
    near_blocks = blocks_of(rows, [depth] * 8, 0)
    sep_only = [o1_sep, y3_sep, k_o1_sep, k_y3_sep]
    sep_blocks = blocks_of(depth, [0] * 16, 16)
    values, near_heads = early(
        place,
        sep_bias,
        head_bias,
        own_values,
        m0,
        near_pieces + far_pieces + sep_only,
        sep_blocks,
        near_blocks,
    )
    m1, y3, k_o1, values, near_heads = tied(m1, y3, k_o1, values, near_heads)

    k_y3 = send(y3, across_cores)
    far_blocks = blocks_of(rows, [depth] * 4 + [0] * 4, 8)
    return finish(
        place,
        sep_bias,
        head_bias,
        strand_pair,
        [values, m1, near_heads],
        near_pieces + far_pieces + sep_only + [o1_head, y3, k_o1, k_y3],
        sep_blocks,
        near_blocks,
        [(i + 8 if i < 4 else i + 12, *block) for i, *block in far_blocks],
    )[None]


def plain_features_kernel(own, other, weight, bias, out):
    bins = own.shape[0]
    for place, part in enumerate((own, other)):
        product = jnp.dot(part[...], weight[...], preferred_element_type=jnp.float32)
        out[pl.ds(place * bins, bins), :] = jax.nn.gelu(
            product + bias[...], approximate=True
        ).astype(jnp.bfloat16)


def plain_features(own, other, weight, bias):
    bins, width = own.shape
    step = 256
    whole = pl.BlockSpec((bins, width), lambda j: (0, 0))
    return pl.pallas_call(
        plain_features_kernel,
        grid=(width // step,),
        in_specs=[
            whole,
            whole,
            pl.BlockSpec((width, step), lambda j: (0, j)),
            pl.BlockSpec((1, step), lambda j: (0, j)),
        ],
        out_specs=pl.BlockSpec((2 * bins, step), lambda j: (0, j)),
        out_shape=jax.ShapeDtypeStruct((2 * bins, width), jnp.bfloat16),
        compiler_params=params(),
        name="features",
    )(own, other, weight, bias)


def plain_heads_kernel(values, weight, bias, out):
    product = lax.dot_general(
        values[...], weight[...], (((1,), (1,)), ((), ())), preferred_element_type=jnp.float32
    )
    out[...] = softplus(product + bias[...]).astype(jnp.bfloat16)


def plain_heads(values, weight, bias):
    rows, width = values.shape
    tracks = weight.shape[0]
    step = 256
    return pl.pallas_call(
        plain_heads_kernel,
        grid=(tracks // step,),
        in_specs=[
            pl.BlockSpec((rows, width), lambda j: (0, 0)),
            pl.BlockSpec((step, width), lambda j: (j, 0)),
            pl.BlockSpec((1, step), lambda j: (0, j)),
        ],
        out_specs=pl.BlockSpec((rows, step), lambda j: (0, j)),
        out_shape=jax.ShapeDtypeStruct((rows, tracks), jnp.bfloat16),
        compiler_params=params(),
        name="heads",
    )(values, weight, bias)


def plain_average_kernel(own, other, pair, out):
    tracks = other.shape[1]
    rows = lax.broadcasted_iota(jnp.int32, (tracks, pair.shape[1]), 0)
    chosen = jnp.where(rows == pair[...], 1.0, 0.0).astype(jnp.bfloat16)
    received = jnp.dot(other[...], chosen, preferred_element_type=jnp.float32)
    out[...] = (0.5 * (own[...].astype(jnp.float32) + received)).astype(jnp.bfloat16)


def plain_average(both, pair):
    rows, tracks = both.shape
    bins = rows // 2
    step = 256
    return pl.pallas_call(
        plain_average_kernel,
        grid=(tracks // step,),
        in_specs=[
            pl.BlockSpec((bins, step), lambda j: (0, j)),
            pl.BlockSpec((bins, tracks), lambda j: (1, 0)),
            pl.BlockSpec((1, step), lambda j: (0, j)),
        ],
        out_specs=pl.BlockSpec((bins, step), lambda j: (0, j)),
        out_shape=jax.ShapeDtypeStruct((bins, tracks), jnp.bfloat16),
        compiler_params=params(),
        name="average",
    )(both, both, pair)


def gather_rows(shard):
    batch = lax.axis_size("batch")
    part = shard.shape[0] // batch
    mine = lax.dynamic_slice_in_dim(shard, lax.axis_index("batch") * part, part, axis=0)
    return lax.all_gather(mine, BOTH, axis=0, tiled=True)


def per_device_plain(
    coarse, skip, depth_kernel, sep_weight, sep_bias, head_weight, head_bias, strand_pair
):
    seq, batch = lax.axis_size("seq"), lax.axis_size("batch")
    coarse, skip = coarse[0], skip[0]
    first = edge(coarse[:1], skip[:1])
    last = edge(coarse[-1:], skip[-1:])
    top = send(last, lambda s, b: (s + 1, b) if s + 1 < seq else None)
    bottom = send(first, lambda s, b: (s - 1, b) if s > 0 else None)
    own, flipped = conv(coarse, skip, top, bottom, depth_kernel)
    other = send(flipped, lambda s, b: (seq - 1 - s, (b + batch // 2) % batch))
    values = plain_features(own, other, gather_rows(sep_weight), sep_bias[None])
    both = plain_heads(values, gather_rows(head_weight.T), head_bias[None])
    return plain_average(both, strand_pair[None])[None]


def solution(mesh):
    tree = mesh.shape["seq"] == 16 and mesh.shape["batch"] == 2
    in_specs = (
        P("batch", "seq", None),
        P("batch", "seq", None),
        P(),
        P("seq", None),
        P(),
        P(None, "seq"),
        P(),
        P(),
    )
    out_specs = P("batch", "seq", None)
    return jax.shard_map(
        per_device_tree if tree else per_device_plain,
        mesh=mesh,
        in_specs=in_specs,
        out_specs=out_specs,
        check_vma=False,
    )
```

```python
import functools

import jax
import jax.numpy as jnp
from jax import lax
from jax.experimental import pallas as pl
from jax.experimental.pallas import tpu as pltpu
from jax.sharding import PartitionSpec as P

BOTH = ("seq", "batch")
VMEM_LIMIT = 56 * 1024 * 1024


def params():
    return pltpu.CompilerParams(vmem_limit_bytes=VMEM_LIMIT)


def cost(flops, bytes_accessed):
    return pl.CostEstimate(flops=flops, bytes_accessed=bytes_accessed, transcendentals=0)


def route(seq, batch, move):
    pairs = []
    for s in range(seq):
        for b in range(batch):
            target = move(s, b)
            if target is not None:
                pairs.append((s * batch + b, target[0] * batch + target[1]))
    return pairs


def send(array, move):
    seq, batch = lax.axis_size("seq"), lax.axis_size("batch")
    return lax.ppermute(array, BOTH, route(seq, batch, move))


def one_hot(shape, hit):
    rows = lax.broadcasted_iota(jnp.int32, shape, 0)
    columns = lax.broadcasted_iota(jnp.int32, shape, 1)
    return jnp.where(hit(rows, columns), 1.0, 0.0).astype(jnp.bfloat16)


def conv_kernel(coarse, skip, top, bottom, taps, own, *flipped):
    bins = skip.shape[0]
    spread = one_hot((bins, coarse.shape[0]), lambda r, c: r // 2 == c)
    up = jnp.dot(spread, coarse[...], preferred_element_type=jnp.float32)
    merged = (up + skip[...].astype(jnp.float32)).astype(jnp.bfloat16).astype(jnp.float32)
    row = lax.broadcasted_iota(jnp.int32, merged.shape, 0)
    before = jnp.where(row == 0, top[...].astype(jnp.float32), pltpu.roll(merged, 1, 0))
    after = jnp.where(
        row == bins - 1, bottom[...].astype(jnp.float32), pltpu.roll(merged, bins - 1, 0)
    )
    result = taps[0:1, :] * before + taps[1:2, :] * merged + taps[2:3, :] * after
    result = result.astype(jnp.bfloat16)
    own[...] = result
    mirror = one_hot((bins, bins), lambda r, c: r + c == bins - 1)
    turned = jnp.dot(mirror, result, preferred_element_type=jnp.float32).astype(jnp.bfloat16)
    start = 0
    for part in flipped:
        part[...] = turned[start : start + part.shape[0]]
        start += part.shape[0]


def conv(coarse, skip, top, bottom, taps, cut=()):
    bins, width = skip.shape
    step = 256
    parts = [b - a for a, b in zip((0, *cut), (*cut, bins))]
    column = lambda rows: pl.BlockSpec((rows, step), lambda j: (0, j))
    return pl.pallas_call(
        conv_kernel,
        grid=(width // step,),
        in_specs=[column(coarse.shape[0]), column(bins), column(1), column(1), column(3)],
        out_specs=[column(rows) for rows in (bins, *parts)],
        out_shape=[jax.ShapeDtypeStruct((rows, width), jnp.bfloat16) for rows in (bins, *parts)],
        compiler_params=params(),
        cost_estimate=cost(2 * bins * bins * width, 6 * bins * width),
        name="conv",
    )(coarse, skip, top, bottom, taps)


def softplus(v):
    e = jnp.exp(-jnp.abs(v))
    return jnp.maximum(v, 0.0) + jnp.where(e < 1e-4, e, jnp.log(1.0 + e))


def gelu(v):
    return jax.nn.gelu(v, approximate=True)


def rows_by_rows(values, weight):
    return lax.dot_general(
        values, weight, (((1,), (1,)), ((), ())), preferred_element_type=jnp.float32
    )


def copies_of(blocks, place, pieces, weight, sems, first):
    copies = []
    for i, (piece, start, rows, slot) in enumerate(blocks):
        target = pl.multiple_of(place[slot] * rows, rows)
        copies.append(
            pltpu.make_async_copy(
                pieces[piece].at[pl.ds(start, rows), :],
                weight.at[pl.ds(target, rows), :],
                sems.at[first + i],
            )
        )
    return copies


def columns_of(j, step):
    return pl.ds(pl.multiple_of(j * step, step), step)


def early_kernel(sep_blocks, near_blocks, place, sep_bias, head_bias, own_values, first, *rest):
    *pieces, values, heads, sep, near, inputs, sems = rest
    bins, part = own_values.shape[0], first.shape[0]
    width, half_tracks = values.shape[1], heads.shape[1]
    which = place[place.shape[0] - 1]
    near_start = pl.multiple_of(which * half_tracks, 128)
    copies = copies_of(sep_blocks, place, pieces, sep, sems, 0)
    near_copies = copies_of(near_blocks, place, pieces, near, sems, len(sep_blocks))
    base = len(sep_blocks) + len(near_blocks)
    copies.append(
        pltpu.make_async_copy(own_values, inputs.at[pl.ds(0, bins), :], sems.at[base])
    )
    copies.append(
        pltpu.make_async_copy(first, inputs.at[pl.ds(bins, part), :], sems.at[base + 1])
    )
    for copy in copies + near_copies:
        copy.start()
    for copy in copies:
        copy.wait()

    @pl.loop(0, width // 256)
    def _(j):
        columns = columns_of(j, 256)
        product = jnp.dot(inputs[...], sep[:, columns], preferred_element_type=jnp.float32)
        values[:, columns] = gelu(product + sep_bias[:, columns]).astype(jnp.bfloat16)

    for copy in near_copies:
        copy.wait()
    step = 384

    @pl.loop(0, half_tracks // step)
    def _(j):
        columns = columns_of(j, step)
        source = pl.ds(pl.multiple_of(near_start + j * step, 128), step)
        product = rows_by_rows(values[...], near[columns, :])
        heads[:, columns] = softplus(product + head_bias[:, source]).astype(jnp.bfloat16)


def early(place, sep_bias, head_bias, own_values, first, pieces, sep_blocks, near_blocks):
    rows, width = own_values.shape[0] + first.shape[0], own_values.shape[1]
    half_tracks = head_bias.shape[1] // 2
    vmem = pl.BlockSpec(memory_space=pltpu.VMEM)
    shapes = [(rows, width), (rows, half_tracks)]
    return pl.pallas_call(
        functools.partial(early_kernel, sep_blocks, near_blocks),
        in_specs=[pl.BlockSpec(memory_space=pltpu.SMEM)]
        + [vmem] * 2
        + [pl.BlockSpec(memory_space=pl.ANY)] * (2 + len(pieces)),
        out_specs=[vmem] * 2,
        out_shape=[jax.ShapeDtypeStruct(shape, jnp.bfloat16) for shape in shapes],
        scratch_shapes=[
            pltpu.VMEM((width, width), jnp.bfloat16),
            pltpu.VMEM((half_tracks, width), jnp.bfloat16),
            pltpu.VMEM((rows, width), jnp.bfloat16),
            pltpu.SemaphoreType.DMA((2 + len(sep_blocks) + len(near_blocks),)),
        ],
        compiler_params=params(),
        cost_estimate=cost(2 * rows * width * (width + half_tracks), 4 * width * width),
        name="early",
    )(place, sep_bias, head_bias, own_values, first, *pieces)


def finish_kernel(sep_blocks, near_blocks, far_blocks, place, sep_bias, head_bias, pair, *rest):
    early_values, later, near_heads, *pieces = rest[:-11]
    out, sep, near, far, last_values, values, own, other, chosen, result, sems = rest[-11:]
    bins, tracks = own.shape
    part = early_values.shape[0] - bins
    width = values.shape[1]
    half_tracks = tracks // 2
    which = place[place.shape[0] - 1]
    near_start = pl.multiple_of(which * half_tracks, 128)
    far_start = pl.multiple_of((1 - which) * half_tracks, 128)
    near_columns = pl.ds(near_start, half_tracks)
    near_first = len(sep_blocks)
    far_first = near_first + len(near_blocks)
    base = far_first + len(far_blocks)

    def fetch(source, target, number):
        copy = pltpu.make_async_copy(source, target, sems.at[base + number])
        copy.start()
        return copy

    later_copy = fetch(later, last_values, 0)
    sep_copies = copies_of(sep_blocks, place, pieces, sep, sems, 0)
    near_copies = copies_of(near_blocks, place, pieces, near, sems, near_first)
    far_copies = copies_of(far_blocks, place, pieces, far, sems, far_first)
    for copy in sep_copies + near_copies:
        copy.start()
    values_copy = fetch(early_values, values.at[pl.ds(0, bins + part), :], 1)
    for copy in far_copies:
        copy.start()
    own_near_copy = fetch(near_heads.at[pl.ds(0, bins), :], own.at[:, near_columns], 2)
    first_near_copy = fetch(
        near_heads.at[pl.ds(bins, part), :], other.at[pl.ds(0, part), near_columns], 3
    )
    later_copy.wait()
    for copy in sep_copies:
        copy.wait()

    @pl.loop(0, width // 256)
    def _(j):
        columns = columns_of(j, 256)
        product = jnp.dot(
            last_values[...], sep[:, columns], preferred_element_type=jnp.float32
        )
        values[bins + part :, columns] = gelu(product + sep_bias[:, columns]).astype(
            jnp.bfloat16
        )

    step = 384
    for copy in near_copies:
        copy.wait()

    @pl.loop(0, half_tracks // step)
    def _(j):
        columns = columns_of(j, step)
        target = pl.ds(pl.multiple_of(near_start + j * step, 128), step)
        product = rows_by_rows(values[bins + part :, :], near[columns, :])
        other[part:, target] = softplus(product + head_bias[:, target]).astype(jnp.bfloat16)

    values_copy.wait()
    for copy in far_copies:
        copy.wait()

    @pl.loop(0, half_tracks // step)
    def _(j):
        columns = columns_of(j, step)
        target = pl.ds(pl.multiple_of(far_start + j * step, 128), step)
        product = rows_by_rows(values[...], far[columns, :])
        heads = softplus(product + head_bias[:, target]).astype(jnp.bfloat16)
        own[:, target] = heads[:bins]
        other[:, target] = heads[bins:]

    own_near_copy.wait()
    first_near_copy.wait()
    step = 256

    def choose(j, slot):
        rows = lax.broadcasted_iota(jnp.int32, (tracks, step), 0)
        hit = rows == pair[:, columns_of(j, step)]
        chosen[slot] = jnp.where(hit, 1.0, 0.0).astype(jnp.bfloat16)

    def result_copy(j):
        columns = columns_of(j, step)
        return pltpu.make_async_copy(
            result.at[:, columns], out.at[:, columns], sems.at[base + 4 + j]
        )

    def combine(j, slot):
        columns = columns_of(j, step)
        received = jnp.dot(other[...], chosen[slot], preferred_element_type=jnp.float32)
        average = 0.5 * (own[:, columns].astype(jnp.float32) + received)
        result[:, columns] = average.astype(jnp.bfloat16)
        result_copy(j).start()

    last = tracks // step - 1
    choose(0, 0)

    @pl.loop(0, last // 2)
    def _(i):
        combine(2 * i, 0)
        choose(2 * i + 1, 1)
        combine(2 * i + 1, 1)
        choose(2 * i + 2, 0)

    if last % 2:
        combine(last - 1, 0)
        choose(last, 1)
    combine(last, last % 2)
    for j in range(last + 1):
        result_copy(j).wait()


def finish(place, sep_bias, head_bias, pair, arrays, pieces, sep_blocks, near_blocks, far_blocks):
    last, width = arrays[1].shape
    bins = (arrays[0].shape[0] + last) // 2
    tracks = head_bias.shape[1]
    vmem = pl.BlockSpec(memory_space=pltpu.VMEM)
    anywhere = pl.BlockSpec(memory_space=pl.ANY)
    bf16 = lambda *shape: pltpu.VMEM(shape, jnp.bfloat16)
    count = len(sep_blocks) + len(near_blocks) + len(far_blocks) + 4 + tracks // 256
    return pl.pallas_call(
        functools.partial(finish_kernel, sep_blocks, near_blocks, far_blocks),
        in_specs=[pl.BlockSpec(memory_space=pltpu.SMEM)]
        + [vmem] * 3
        + [anywhere] * (len(arrays) + len(pieces)),
        out_specs=anywhere,
        out_shape=jax.ShapeDtypeStruct((bins, tracks), jnp.bfloat16),
        scratch_shapes=[
            bf16(width, width),
            bf16(tracks // 2, width),
            bf16(tracks // 2, width),
            bf16(last, width),
            bf16(2 * bins, width),
            bf16(bins, tracks),
            bf16(bins, tracks),
            bf16(2, tracks, 256),
            bf16(bins, tracks),
            pltpu.SemaphoreType.DMA((count,)),
        ],
        compiler_params=params(),
        cost_estimate=cost(8 * bins * tracks * tracks, 16 * bins * tracks),
        name="finish",
    )(place, sep_bias, head_bias, pair, *arrays, *pieces)


def along_line(s, b):
    return s ^ 4, b


def across_middle(s, b):
    return ((3 - s // 4) * 4 + s % 4, b) if s // 4 in (1, 2) else None


def to_line_ends(s, b):
    return (s ^ 4, b) if s // 4 in (1, 2) else None


def across_pair(s, b):
    return s ^ 2, b


def across_cores(s, b):
    return s ^ 1, b


def blocks_of(rows, starts, first):
    return [(i, start, rows, first + i) for i, start in enumerate(starts)]


def places():
    s = lax.axis_index("seq")
    z, y, c = s // 4, (s // 2) % 2, s % 2
    inner = jnp.where(z < 2, 2, 1)
    within, among = [], []
    for zz in (z, z ^ 1, inner, inner ^ 1):
        for core in (c, 1 - c):
            for yy in (y, 1 - y):
                within.append((zz % 2) * 4 + yy * 2 + core)
                among.append(zz * 4 + yy * 2 + core)
    return jnp.stack(within + among + [s // 8]).astype(jnp.int32)


def edge(coarse_row, skip_row):
    total = coarse_row.astype(jnp.float32) + skip_row.astype(jnp.float32)
    return total.astype(jnp.bfloat16)


def tied(*trees):
    return lax.optimization_barrier(trees)


def per_device_tree(
    coarse, skip, depth_kernel, sep_weight, sep_bias, head_weight, head_bias, strand_pair
):
    seq, batch = lax.axis_size("seq"), lax.axis_size("batch")
    coarse, skip = coarse[0], skip[0]
    first = edge(coarse[:1], skip[:1])
    last = edge(coarse[-1:], skip[-1:])
    even = lax.axis_index("seq") % 2 == 0
    inside = send(jnp.where(even, last, first), across_cores)
    outside = send(
        jnp.where(even, first, last),
        lambda s, b: (s + 2 * (s % 2) - 1, b) if 0 <= s + 2 * (s % 2) - 1 < seq else None,
    )
    to_mirror = lambda s, b: (seq - 1 - s, (b + batch // 2) % batch)
    z = lax.axis_index("seq") // 4
    pick = lambda a, c: jnp.where((z == 1) | (z == 2), a, c)

    own = jnp.concatenate([sep_weight, head_weight.T])
    near = send(own, along_line)
    q0 = send(own, across_middle)
    y0 = send(own, across_pair)
    k_own = send(own, across_cores)
    small = (sep_bias, head_bias, strand_pair)
    edges = (inside, outside)
    near, q0, y0, k_own, edges, small = tied(near, q0, y0, k_own, edges, small)
    sep_bias, head_bias, strand_pair = small

    inside, outside = edges
    top, bottom = jnp.where(even, outside, inside), jnp.where(even, inside, outside)
    own_values, *flipped = conv(coarse, skip, top, bottom, depth_kernel, (5 * skip.shape[0] // 8,))
    q1 = send(near, across_middle)
    y1 = send(near, across_pair)
    s0 = send(q0, to_line_ends)
    k_y0 = send(y0, across_cores)
    k_near = send(near, across_cores)
    small = (sep_bias[None], head_bias[None], strand_pair[None], places())
    q1, y1, s0, k_y0, k_near, flipped, own_values, small = tied(
        q1, y1, s0, k_y0, k_near, flipped, own_values, small
    )
    sep_bias, head_bias, strand_pair, place = small

    m0 = send(flipped[0], to_mirror)
    o0 = pick(q0, s0)
    y2 = send(o0, across_pair)
    s1 = send(q1, to_line_ends)
    k_y1 = send(y1, across_cores)
    k_o0 = send(o0, across_cores)
    m0, y2, s1, k_y1, k_o0, flipped = tied(m0, y2, s1, k_y1, k_o0, flipped)

    depth = sep_weight.shape[0]
    o1_sep, o1_head = pick(q1[:depth], s1[:depth]), pick(q1[depth:], s1[depth:])
    y3_sep = send(o1_sep, across_pair)
    k_y2 = send(y2, across_cores)
    k_o1_sep = send(o1_sep, across_cores)
    y3_sep, o1_head, last_part = tied(y3_sep, o1_head, flipped[1])

    m1 = send(last_part, to_mirror)
    y3 = send(o1_head, across_pair)
    k_y3_sep = send(y3_sep, across_cores)
    k_o1 = send(o1_head, across_cores)
    near_pieces = [own, y0, k_own, k_y0, near, y1, k_near, k_y1]
    far_pieces = [o0, y2, k_o0, k_y2]
    rows = own.shape[0] - depth
    near_blocks = blocks_of(rows, [depth] * 8, 0)
    sep_only = [o1_sep, y3_sep, k_o1_sep, k_y3_sep]
    sep_blocks = blocks_of(depth, [0] * 16, 16)
    values, near_heads = early(
        place,
        sep_bias,
        head_bias,
        own_values,
        m0,
        near_pieces + far_pieces + sep_only,
        sep_blocks,
        near_blocks,
    )
    m1, y3, k_o1, values, near_heads = tied(m1, y3, k_o1, values, near_heads)

    k_y3 = send(y3, across_cores)
    far_blocks = blocks_of(rows, [depth] * 4 + [0] * 4, 8)
    return finish(
        place,
        sep_bias,
        head_bias,
        strand_pair,
        [values, m1, near_heads],
        near_pieces + far_pieces + sep_only + [o1_head, y3, k_o1, k_y3],
        sep_blocks,
        near_blocks,
        [(i + 8 if i < 4 else i + 12, *block) for i, *block in far_blocks],
    )[None]


def plain_features_kernel(own, other, weight, bias, out):
    bins = own.shape[0]
    for place, part in enumerate((own, other)):
        product = jnp.dot(part[...], weight[...], preferred_element_type=jnp.float32)
        out[pl.ds(place * bins, bins), :] = jax.nn.gelu(
            product + bias[...], approximate=True
        ).astype(jnp.bfloat16)


def plain_features(own, other, weight, bias):
    bins, width = own.shape
    step = 256
    whole = pl.BlockSpec((bins, width), lambda j: (0, 0))
    return pl.pallas_call(
        plain_features_kernel,
        grid=(width // step,),
        in_specs=[
            whole,
            whole,
            pl.BlockSpec((width, step), lambda j: (0, j)),
            pl.BlockSpec((1, step), lambda j: (0, j)),
        ],
        out_specs=pl.BlockSpec((2 * bins, step), lambda j: (0, j)),
        out_shape=jax.ShapeDtypeStruct((2 * bins, width), jnp.bfloat16),
        compiler_params=params(),
        name="features",
    )(own, other, weight, bias)


def plain_heads_kernel(values, weight, bias, out):
    product = lax.dot_general(
        values[...], weight[...], (((1,), (1,)), ((), ())), preferred_element_type=jnp.float32
    )
    out[...] = softplus(product + bias[...]).astype(jnp.bfloat16)


def plain_heads(values, weight, bias):
    rows, width = values.shape
    tracks = weight.shape[0]
    step = 256
    return pl.pallas_call(
        plain_heads_kernel,
        grid=(tracks // step,),
        in_specs=[
            pl.BlockSpec((rows, width), lambda j: (0, 0)),
            pl.BlockSpec((step, width), lambda j: (j, 0)),
            pl.BlockSpec((1, step), lambda j: (0, j)),
        ],
        out_specs=pl.BlockSpec((rows, step), lambda j: (0, j)),
        out_shape=jax.ShapeDtypeStruct((rows, tracks), jnp.bfloat16),
        compiler_params=params(),
        name="heads",
    )(values, weight, bias)


def plain_average_kernel(own, other, pair, out):
    tracks = other.shape[1]
    rows = lax.broadcasted_iota(jnp.int32, (tracks, pair.shape[1]), 0)
    chosen = jnp.where(rows == pair[...], 1.0, 0.0).astype(jnp.bfloat16)
    received = jnp.dot(other[...], chosen, preferred_element_type=jnp.float32)
    out[...] = (0.5 * (own[...].astype(jnp.float32) + received)).astype(jnp.bfloat16)


def plain_average(both, pair):
    rows, tracks = both.shape
    bins = rows // 2
    step = 256
    return pl.pallas_call(
        plain_average_kernel,
        grid=(tracks // step,),
        in_specs=[
            pl.BlockSpec((bins, step), lambda j: (0, j)),
            pl.BlockSpec((bins, tracks), lambda j: (1, 0)),
            pl.BlockSpec((1, step), lambda j: (0, j)),
        ],
        out_specs=pl.BlockSpec((bins, step), lambda j: (0, j)),
        out_shape=jax.ShapeDtypeStruct((bins, tracks), jnp.bfloat16),
        compiler_params=params(),
        name="average",
    )(both, both, pair)


def gather_rows(shard):
    batch = lax.axis_size("batch")
    part = shard.shape[0] // batch
    mine = lax.dynamic_slice_in_dim(shard, lax.axis_index("batch") * part, part, axis=0)
    return lax.all_gather(mine, BOTH, axis=0, tiled=True)


def per_device_plain(
    coarse, skip, depth_kernel, sep_weight, sep_bias, head_weight, head_bias, strand_pair
):
    seq, batch = lax.axis_size("seq"), lax.axis_size("batch")
    coarse, skip = coarse[0], skip[0]
    first = edge(coarse[:1], skip[:1])
    last = edge(coarse[-1:], skip[-1:])
    top = send(last, lambda s, b: (s + 1, b) if s + 1 < seq else None)
    bottom = send(first, lambda s, b: (s - 1, b) if s > 0 else None)
    own, flipped = conv(coarse, skip, top, bottom, depth_kernel)
    other = send(flipped, lambda s, b: (seq - 1 - s, (b + batch // 2) % batch))
    values = plain_features(own, other, gather_rows(sep_weight), sep_bias[None])
    both = plain_heads(values, gather_rows(head_weight.T), head_bias[None])
    return plain_average(both, strand_pair[None])[None]


def solution(mesh):
    tree = mesh.shape["seq"] == 16 and mesh.shape["batch"] == 2
    in_specs = (
        P("batch", "seq", None),
        P("batch", "seq", None),
        P(),
        P("seq", None),
        P(),
        P(None, "seq"),
        P(),
        P(),
    )
    out_specs = P("batch", "seq", None)
    return jax.shard_map(
        per_device_tree if tree else per_device_plain,
        mesh=mesh,
        in_specs=in_specs,
        out_specs=out_specs,
        check_vma=False,
    )
```

```python
import functools

import jax
import jax.numpy as jnp
from jax import lax
from jax.experimental import pallas as pl
from jax.experimental.pallas import tpu as pltpu
from jax.sharding import PartitionSpec as P

BOTH = ("seq", "batch")
VMEM_LIMIT = 56 * 1024 * 1024


def params():
    return pltpu.CompilerParams(vmem_limit_bytes=VMEM_LIMIT)


def cost(flops, bytes_accessed):
    return pl.CostEstimate(flops=flops, bytes_accessed=bytes_accessed, transcendentals=0)


def route(seq, batch, move):
    pairs = []
    for s in range(seq):
        for b in range(batch):
            target = move(s, b)
            if target is not None:
                pairs.append((s * batch + b, target[0] * batch + target[1]))
    return pairs


def send(array, move):
    seq, batch = lax.axis_size("seq"), lax.axis_size("batch")
    return lax.ppermute(array, BOTH, route(seq, batch, move))


def one_hot(shape, hit):
    rows = lax.broadcasted_iota(jnp.int32, shape, 0)
    columns = lax.broadcasted_iota(jnp.int32, shape, 1)
    return jnp.where(hit(rows, columns), 1.0, 0.0).astype(jnp.bfloat16)


def conv_kernel(coarse, skip, top, bottom, taps, own, *flipped):
    bins = skip.shape[0]
    spread = one_hot((bins, coarse.shape[0]), lambda r, c: r // 2 == c)
    up = jnp.dot(spread, coarse[...], preferred_element_type=jnp.float32)
    merged = (up + skip[...].astype(jnp.float32)).astype(jnp.bfloat16).astype(jnp.float32)
    row = lax.broadcasted_iota(jnp.int32, merged.shape, 0)
    before = jnp.where(row == 0, top[...].astype(jnp.float32), pltpu.roll(merged, 1, 0))
    after = jnp.where(
        row == bins - 1, bottom[...].astype(jnp.float32), pltpu.roll(merged, bins - 1, 0)
    )
    result = taps[0:1, :] * before + taps[1:2, :] * merged + taps[2:3, :] * after
    result = result.astype(jnp.bfloat16)
    own[...] = result
    mirror = one_hot((bins, bins), lambda r, c: r + c == bins - 1)
    turned = jnp.dot(mirror, result, preferred_element_type=jnp.float32).astype(jnp.bfloat16)
    start = 0
    for part in flipped:
        part[...] = turned[start : start + part.shape[0]]
        start += part.shape[0]


def conv(coarse, skip, top, bottom, taps, cut=()):
    bins, width = skip.shape
    step = 256
    parts = [b - a for a, b in zip((0, *cut), (*cut, bins))]
    column = lambda rows: pl.BlockSpec((rows, step), lambda j: (0, j))
    return pl.pallas_call(
        conv_kernel,
        grid=(width // step,),
        in_specs=[column(coarse.shape[0]), column(bins), column(1), column(1), column(3)],
        out_specs=[column(rows) for rows in (bins, *parts)],
        out_shape=[jax.ShapeDtypeStruct((rows, width), jnp.bfloat16) for rows in (bins, *parts)],
        compiler_params=params(),
        cost_estimate=cost(2 * bins * bins * width, 6 * bins * width),
        name="conv",
    )(coarse, skip, top, bottom, taps)


def softplus(v):
    e = jnp.exp(-jnp.abs(v))
    return jnp.maximum(v, 0.0) + jnp.where(e < 1e-4, e, jnp.log(1.0 + e))


def gelu(v):
    return jax.nn.gelu(v, approximate=True)


def rows_by_rows(values, weight):
    return lax.dot_general(
        values, weight, (((1,), (1,)), ((), ())), preferred_element_type=jnp.float32
    )


def copies_of(blocks, place, pieces, weight, sems, first):
    copies = []
    for i, (piece, start, rows, slot) in enumerate(blocks):
        target = pl.multiple_of(place[slot] * rows, rows)
        copies.append(
            pltpu.make_async_copy(
                pieces[piece].at[pl.ds(start, rows), :],
                weight.at[pl.ds(target, rows), :],
                sems.at[first + i],
            )
        )
    return copies


def columns_of(j, step):
    return pl.ds(pl.multiple_of(j * step, step), step)


def early_kernel(sep_blocks, near_blocks, place, sep_bias, head_bias, own_values, first, *rest):
    *pieces, values, heads, sep, near, inputs, sems = rest
    bins, part = own_values.shape[0], first.shape[0]
    width, half_tracks = values.shape[1], heads.shape[1]
    which = place[place.shape[0] - 1]
    near_start = pl.multiple_of(which * half_tracks, 128)
    copies = copies_of(sep_blocks, place, pieces, sep, sems, 0)
    near_copies = copies_of(near_blocks, place, pieces, near, sems, len(sep_blocks))
    base = len(sep_blocks) + len(near_blocks)
    copies.append(
        pltpu.make_async_copy(own_values, inputs.at[pl.ds(0, bins), :], sems.at[base])
    )
    copies.append(
        pltpu.make_async_copy(first, inputs.at[pl.ds(bins, part), :], sems.at[base + 1])
    )
    for copy in copies + near_copies:
        copy.start()
    for copy in copies:
        copy.wait()

    @pl.loop(0, width // 256)
    def _(j):
        columns = columns_of(j, 256)
        product = jnp.dot(inputs[...], sep[:, columns], preferred_element_type=jnp.float32)
        values[:, columns] = gelu(product + sep_bias[:, columns]).astype(jnp.bfloat16)

    for copy in near_copies:
        copy.wait()
    step = 384

    @pl.loop(0, half_tracks // step)
    def _(j):
        columns = columns_of(j, step)
        source = pl.ds(pl.multiple_of(near_start + j * step, 128), step)
        product = rows_by_rows(values[...], near[columns, :])
        heads[:, columns] = softplus(product + head_bias[:, source]).astype(jnp.bfloat16)


def early(place, sep_bias, head_bias, own_values, first, pieces, sep_blocks, near_blocks):
    rows, width = own_values.shape[0] + first.shape[0], own_values.shape[1]
    half_tracks = head_bias.shape[1] // 2
    vmem = pl.BlockSpec(memory_space=pltpu.VMEM)
    shapes = [(rows, width), (rows, half_tracks)]
    return pl.pallas_call(
        functools.partial(early_kernel, sep_blocks, near_blocks),
        in_specs=[pl.BlockSpec(memory_space=pltpu.SMEM)]
        + [vmem] * 2
        + [pl.BlockSpec(memory_space=pl.ANY)] * (2 + len(pieces)),
        out_specs=[vmem] * 2,
        out_shape=[jax.ShapeDtypeStruct(shape, jnp.bfloat16) for shape in shapes],
        scratch_shapes=[
            pltpu.VMEM((width, width), jnp.bfloat16),
            pltpu.VMEM((half_tracks, width), jnp.bfloat16),
            pltpu.VMEM((rows, width), jnp.bfloat16),
            pltpu.SemaphoreType.DMA((2 + len(sep_blocks) + len(near_blocks),)),
        ],
        compiler_params=params(),
        cost_estimate=cost(2 * rows * width * (width + half_tracks), 4 * width * width),
        name="early",
    )(place, sep_bias, head_bias, own_values, first, *pieces)


def finish_kernel(sep_blocks, near_blocks, far_blocks, place, sep_bias, head_bias, pair, *rest):
    early_values, later, near_heads, *pieces = rest[:-11]
    out, sep, near, far, last_values, values, own, other, chosen, result, sems = rest[-11:]
    bins, tracks = own.shape
    part = early_values.shape[0] - bins
    width = values.shape[1]
    half_tracks = tracks // 2
    which = place[place.shape[0] - 1]
    near_start = pl.multiple_of(which * half_tracks, 128)
    far_start = pl.multiple_of((1 - which) * half_tracks, 128)
    near_columns = pl.ds(near_start, half_tracks)
    near_first = len(sep_blocks)
    far_first = near_first + len(near_blocks)
    base = far_first + len(far_blocks)

    def fetch(source, target, number):
        copy = pltpu.make_async_copy(source, target, sems.at[base + number])
        copy.start()
        return copy

    later_copy = fetch(later, last_values, 0)
    sep_copies = copies_of(sep_blocks, place, pieces, sep, sems, 0)
    near_copies = copies_of(near_blocks, place, pieces, near, sems, near_first)
    far_copies = copies_of(far_blocks, place, pieces, far, sems, far_first)
    for copy in sep_copies + near_copies:
        copy.start()
    values_copy = fetch(early_values, values.at[pl.ds(0, bins + part), :], 1)
    for copy in far_copies:
        copy.start()
    own_near_copy = fetch(near_heads.at[pl.ds(0, bins), :], own.at[:, near_columns], 2)
    first_near_copy = fetch(
        near_heads.at[pl.ds(bins, part), :], other.at[pl.ds(0, part), near_columns], 3
    )
    later_copy.wait()
    for copy in sep_copies:
        copy.wait()

    @pl.loop(0, width // 256)
    def _(j):
        columns = columns_of(j, 256)
        product = jnp.dot(
            last_values[...], sep[:, columns], preferred_element_type=jnp.float32
        )
        values[bins + part :, columns] = gelu(product + sep_bias[:, columns]).astype(
            jnp.bfloat16
        )

    for copy in near_copies:
        copy.wait()

    def in_blocks(body):
        step = 256
        full = half_tracks // step

        @pl.loop(0, full)
        def _(j):
            body(pl.multiple_of(j * step, step), step)

        if half_tracks % step:
            body(full * step, half_tracks % step)

    @in_blocks
    def _(start, size):
        columns = pl.ds(start, size)
        target = pl.ds(pl.multiple_of(near_start + start, 128), size)
        product = rows_by_rows(values[bins + part :, :], near[columns, :])
        other[part:, target] = softplus(product + head_bias[:, target]).astype(jnp.bfloat16)

    values_copy.wait()
    for copy in far_copies:
        copy.wait()

    @in_blocks
    def _(start, size):
        columns = pl.ds(start, size)
        target = pl.ds(pl.multiple_of(far_start + start, 128), size)
        product = rows_by_rows(values[...], far[columns, :])
        heads = softplus(product + head_bias[:, target]).astype(jnp.bfloat16)
        own[:, target] = heads[:bins]
        other[:, target] = heads[bins:]

    own_near_copy.wait()
    first_near_copy.wait()
    step = 256

    def choose(j, slot):
        rows = lax.broadcasted_iota(jnp.int32, (tracks, step), 0)
        hit = rows == pair[:, columns_of(j, step)]
        chosen[slot] = jnp.where(hit, 1.0, 0.0).astype(jnp.bfloat16)

    def result_copy(j):
        columns = columns_of(j, step)
        return pltpu.make_async_copy(
            result.at[:, columns], out.at[:, columns], sems.at[base + 4 + j]
        )

    def combine(j, slot):
        columns = columns_of(j, step)
        received = jnp.dot(other[...], chosen[slot], preferred_element_type=jnp.float32)
        average = 0.5 * (own[:, columns].astype(jnp.float32) + received)
        result[:, columns] = average.astype(jnp.bfloat16)
        result_copy(j).start()

    last = tracks // step - 1
    choose(0, 0)

    @pl.loop(0, last // 2)
    def _(i):
        combine(2 * i, 0)
        choose(2 * i + 1, 1)
        combine(2 * i + 1, 1)
        choose(2 * i + 2, 0)

    if last % 2:
        combine(last - 1, 0)
        choose(last, 1)
    combine(last, last % 2)
    for j in range(last + 1):
        result_copy(j).wait()


def finish(place, sep_bias, head_bias, pair, arrays, pieces, sep_blocks, near_blocks, far_blocks):
    last, width = arrays[1].shape
    bins = (arrays[0].shape[0] + last) // 2
    tracks = head_bias.shape[1]
    vmem = pl.BlockSpec(memory_space=pltpu.VMEM)
    anywhere = pl.BlockSpec(memory_space=pl.ANY)
    bf16 = lambda *shape: pltpu.VMEM(shape, jnp.bfloat16)
    count = len(sep_blocks) + len(near_blocks) + len(far_blocks) + 4 + tracks // 256
    return pl.pallas_call(
        functools.partial(finish_kernel, sep_blocks, near_blocks, far_blocks),
        in_specs=[pl.BlockSpec(memory_space=pltpu.SMEM)]
        + [vmem] * 3
        + [anywhere] * (len(arrays) + len(pieces)),
        out_specs=anywhere,
        out_shape=jax.ShapeDtypeStruct((bins, tracks), jnp.bfloat16),
        scratch_shapes=[
            bf16(width, width),
            bf16(tracks // 2, width),
            bf16(tracks // 2, width),
            bf16(last, width),
            bf16(2 * bins, width),
            bf16(bins, tracks),
            bf16(bins, tracks),
            bf16(2, tracks, 256),
            bf16(bins, tracks),
            pltpu.SemaphoreType.DMA((count,)),
        ],
        compiler_params=params(),
        cost_estimate=cost(8 * bins * tracks * tracks, 16 * bins * tracks),
        name="finish",
    )(place, sep_bias, head_bias, pair, *arrays, *pieces)


def along_line(s, b):
    return s ^ 4, b


def across_middle(s, b):
    return ((3 - s // 4) * 4 + s % 4, b) if s // 4 in (1, 2) else None


def to_line_ends(s, b):
    return (s ^ 4, b) if s // 4 in (1, 2) else None


def across_pair(s, b):
    return s ^ 2, b


def across_cores(s, b):
    return s ^ 1, b


def blocks_of(rows, starts, first):
    return [(i, start, rows, first + i) for i, start in enumerate(starts)]


def places():
    s = lax.axis_index("seq")
    z, y, c = s // 4, (s // 2) % 2, s % 2
    inner = jnp.where(z < 2, 2, 1)
    within, among = [], []
    for zz in (z, z ^ 1, inner, inner ^ 1):
        for core in (c, 1 - c):
            for yy in (y, 1 - y):
                within.append((zz % 2) * 4 + yy * 2 + core)
                among.append(zz * 4 + yy * 2 + core)
    return jnp.stack(within + among + [s // 8]).astype(jnp.int32)


def edge(coarse_row, skip_row):
    total = coarse_row.astype(jnp.float32) + skip_row.astype(jnp.float32)
    return total.astype(jnp.bfloat16)


def tied(*trees):
    return lax.optimization_barrier(trees)


def per_device_tree(
    coarse, skip, depth_kernel, sep_weight, sep_bias, head_weight, head_bias, strand_pair
):
    seq, batch = lax.axis_size("seq"), lax.axis_size("batch")
    coarse, skip = coarse[0], skip[0]
    first = edge(coarse[:1], skip[:1])
    last = edge(coarse[-1:], skip[-1:])
    even = lax.axis_index("seq") % 2 == 0
    inside = send(jnp.where(even, last, first), across_cores)
    outside = send(
        jnp.where(even, first, last),
        lambda s, b: (s + 2 * (s % 2) - 1, b) if 0 <= s + 2 * (s % 2) - 1 < seq else None,
    )
    to_mirror = lambda s, b: (seq - 1 - s, (b + batch // 2) % batch)
    z = lax.axis_index("seq") // 4
    pick = lambda a, c: jnp.where((z == 1) | (z == 2), a, c)

    own = jnp.concatenate([sep_weight, head_weight.T])
    near = send(own, along_line)
    q0 = send(own, across_middle)
    y0 = send(own, across_pair)
    k_own = send(own, across_cores)
    small = (sep_bias, head_bias, strand_pair)
    edges = (inside, outside)
    near, q0, y0, k_own, edges, small = tied(near, q0, y0, k_own, edges, small)
    sep_bias, head_bias, strand_pair = small

    inside, outside = edges
    top, bottom = jnp.where(even, outside, inside), jnp.where(even, inside, outside)
    own_values, *flipped = conv(coarse, skip, top, bottom, depth_kernel, (5 * skip.shape[0] // 8,))
    q1 = send(near, across_middle)
    y1 = send(near, across_pair)
    s0 = send(q0, to_line_ends)
    k_y0 = send(y0, across_cores)
    k_near = send(near, across_cores)
    small = (sep_bias[None], head_bias[None], strand_pair[None], places())
    q1, y1, s0, k_y0, k_near, flipped, own_values, small = tied(
        q1, y1, s0, k_y0, k_near, flipped, own_values, small
    )
    sep_bias, head_bias, strand_pair, place = small

    m0 = send(flipped[0], to_mirror)
    o0 = pick(q0, s0)
    y2 = send(o0, across_pair)
    s1 = send(q1, to_line_ends)
    k_y1 = send(y1, across_cores)
    k_o0 = send(o0, across_cores)
    m0, y2, s1, k_y1, k_o0, flipped = tied(m0, y2, s1, k_y1, k_o0, flipped)

    depth = sep_weight.shape[0]
    o1_sep, o1_head = pick(q1[:depth], s1[:depth]), pick(q1[depth:], s1[depth:])
    y3_sep = send(o1_sep, across_pair)
    k_y2 = send(y2, across_cores)
    k_o1_sep = send(o1_sep, across_cores)
    y3_sep, o1_head, last_part = tied(y3_sep, o1_head, flipped[1])

    m1 = send(last_part, to_mirror)
    y3 = send(o1_head, across_pair)
    k_y3_sep = send(y3_sep, across_cores)
    k_o1 = send(o1_head, across_cores)
    near_pieces = [own, y0, k_own, k_y0, near, y1, k_near, k_y1]
    far_pieces = [o0, y2, k_o0, k_y2]
    rows = own.shape[0] - depth
    near_blocks = blocks_of(rows, [depth] * 8, 0)
    sep_only = [o1_sep, y3_sep, k_o1_sep, k_y3_sep]
    sep_blocks = blocks_of(depth, [0] * 16, 16)
    values, near_heads = early(
        place,
        sep_bias,
        head_bias,
        own_values,
        m0,
        near_pieces + far_pieces + sep_only,
        sep_blocks,
        near_blocks,
    )
    m1, y3, k_o1, values, near_heads = tied(m1, y3, k_o1, values, near_heads)

    k_y3 = send(y3, across_cores)
    far_blocks = blocks_of(rows, [depth] * 4 + [0] * 4, 8)
    return finish(
        place,
        sep_bias,
        head_bias,
        strand_pair,
        [values, m1, near_heads],
        near_pieces + far_pieces + sep_only + [o1_head, y3, k_o1, k_y3],
        sep_blocks,
        near_blocks,
        [(i + 8 if i < 4 else i + 12, *block) for i, *block in far_blocks],
    )[None]


def plain_features_kernel(own, other, weight, bias, out):
    bins = own.shape[0]
    for place, part in enumerate((own, other)):
        product = jnp.dot(part[...], weight[...], preferred_element_type=jnp.float32)
        out[pl.ds(place * bins, bins), :] = jax.nn.gelu(
            product + bias[...], approximate=True
        ).astype(jnp.bfloat16)


def plain_features(own, other, weight, bias):
    bins, width = own.shape
    step = 256
    whole = pl.BlockSpec((bins, width), lambda j: (0, 0))
    return pl.pallas_call(
        plain_features_kernel,
        grid=(width // step,),
        in_specs=[
            whole,
            whole,
            pl.BlockSpec((width, step), lambda j: (0, j)),
            pl.BlockSpec((1, step), lambda j: (0, j)),
        ],
        out_specs=pl.BlockSpec((2 * bins, step), lambda j: (0, j)),
        out_shape=jax.ShapeDtypeStruct((2 * bins, width), jnp.bfloat16),
        compiler_params=params(),
        name="features",
    )(own, other, weight, bias)


def plain_heads_kernel(values, weight, bias, out):
    product = lax.dot_general(
        values[...], weight[...], (((1,), (1,)), ((), ())), preferred_element_type=jnp.float32
    )
    out[...] = softplus(product + bias[...]).astype(jnp.bfloat16)


def plain_heads(values, weight, bias):
    rows, width = values.shape
    tracks = weight.shape[0]
    step = 256
    return pl.pallas_call(
        plain_heads_kernel,
        grid=(tracks // step,),
        in_specs=[
            pl.BlockSpec((rows, width), lambda j: (0, 0)),
            pl.BlockSpec((step, width), lambda j: (j, 0)),
            pl.BlockSpec((1, step), lambda j: (0, j)),
        ],
        out_specs=pl.BlockSpec((rows, step), lambda j: (0, j)),
        out_shape=jax.ShapeDtypeStruct((rows, tracks), jnp.bfloat16),
        compiler_params=params(),
        name="heads",
    )(values, weight, bias)


def plain_average_kernel(own, other, pair, out):
    tracks = other.shape[1]
    rows = lax.broadcasted_iota(jnp.int32, (tracks, pair.shape[1]), 0)
    chosen = jnp.where(rows == pair[...], 1.0, 0.0).astype(jnp.bfloat16)
    received = jnp.dot(other[...], chosen, preferred_element_type=jnp.float32)
    out[...] = (0.5 * (own[...].astype(jnp.float32) + received)).astype(jnp.bfloat16)


def plain_average(both, pair):
    rows, tracks = both.shape
    bins = rows // 2
    step = 256
    return pl.pallas_call(
        plain_average_kernel,
        grid=(tracks // step,),
        in_specs=[
            pl.BlockSpec((bins, step), lambda j: (0, j)),
            pl.BlockSpec((bins, tracks), lambda j: (1, 0)),
            pl.BlockSpec((1, step), lambda j: (0, j)),
        ],
        out_specs=pl.BlockSpec((bins, step), lambda j: (0, j)),
        out_shape=jax.ShapeDtypeStruct((bins, tracks), jnp.bfloat16),
        compiler_params=params(),
        name="average",
    )(both, both, pair)


def gather_rows(shard):
    batch = lax.axis_size("batch")
    part = shard.shape[0] // batch
    mine = lax.dynamic_slice_in_dim(shard, lax.axis_index("batch") * part, part, axis=0)
    return lax.all_gather(mine, BOTH, axis=0, tiled=True)


def per_device_plain(
    coarse, skip, depth_kernel, sep_weight, sep_bias, head_weight, head_bias, strand_pair
):
    seq, batch = lax.axis_size("seq"), lax.axis_size("batch")
    coarse, skip = coarse[0], skip[0]
    first = edge(coarse[:1], skip[:1])
    last = edge(coarse[-1:], skip[-1:])
    top = send(last, lambda s, b: (s + 1, b) if s + 1 < seq else None)
    bottom = send(first, lambda s, b: (s - 1, b) if s > 0 else None)
    own, flipped = conv(coarse, skip, top, bottom, depth_kernel)
    other = send(flipped, lambda s, b: (seq - 1 - s, (b + batch // 2) % batch))
    values = plain_features(own, other, gather_rows(sep_weight), sep_bias[None])
    both = plain_heads(values, gather_rows(head_weight.T), head_bias[None])
    return plain_average(both, strand_pair[None])[None]


def solution(mesh):
    tree = mesh.shape["seq"] == 16 and mesh.shape["batch"] == 2
    in_specs = (
        P("batch", "seq", None),
        P("batch", "seq", None),
        P(),
        P("seq", None),
        P(),
        P(None, "seq"),
        P(),
        P(),
    )
    out_specs = P("batch", "seq", None)
    return jax.shard_map(
        per_device_tree if tree else per_device_plain,
        mesh=mesh,
        in_specs=in_specs,
        out_specs=out_specs,
        check_vma=False,
    )
```
